512 devices in a mesh: leaf: 128 (over z, y, core), sub: 4 (over x).
Axes of the slice: x: 4, y: 8, z: 8, core: 2. Of those that a mesh axis runs over, the one named last changes fastest.
Arguments:
- points: bfloat16 [8192, 64, 256], P(('leaf', 'sub')), may hold values from -6 to 6
- probe_bits: int32 [8192, 16, 256], P(('leaf', 'sub')), may hold values from 0 to 1
- leaf_skel: int32 [8192, 128], P(('leaf', 'sub')), may hold values from 0 to 255, as said below
- leaf_basis: bfloat16 [8192, 128, 256], P(('leaf', 'sub')), may hold values from -0.4375 to 0.4375
- device_skel: int32 [512, 128], P(('leaf', 'sub')), may hold values from 0 to 2047, as said below
- device_basis: bfloat16 [512, 128, 2048], P(('leaf', 'sub')), may hold values from -0.25 to 0.25
- subtree_skel: int32 [128, 128], P('leaf'), may hold values from 0 to 511, as said below
- subtree_basis: bfloat16 [128, 128, 512], P('leaf'), may hold values from -0.375 to 0.375
- upper_skel: int32 [128, 6, 128], P('leaf'), may hold values from 0 to 255, as said below
- upper_basis: bfloat16 [128, 6, 128, 256], P('leaf'), as said below
- near_pairs: int32 [512, 80, 2], P(('leaf', 'sub')), may hold values from 0 to 63, as said below
- near_count: int32 [512], P(('leaf', 'sub')), may hold values from 1 to 80, 16384 in all
- far_pairs: int32 [512, 96, 2], P(('leaf', 'sub')), may hold values from 0 to 63, as said below
Outputs:
- product: float32 [8192, 16, 256], P(('leaf', 'sub'))
The draws below stay inside these ranges and needn't reach their ends.
Inputs may be any that keep to these rules, and one draw needn't show every extreme that they name: `leaf_skel`: each row names 128 different points of its leaf. `device_skel`: each row names 128 different columns. `subtree_skel`: each row names 128 different columns. `upper_skel`: each row names 128 different columns; entries [g, t-1] are equal for all subtrees g under one node of level t. `upper_basis`: entries [g, t-1] are equal for all subtrees g under one node of level t. `near_pairs`: entry 0 of a row is a leaf of the device (0 to 15), entry 1 a leaf of its subtree numbered 0 to 63 in the subtree, never the first leaf itself; the rows of one device are different pairs. `near_count`: some device has exactly 80 pairs. `far_pairs`: as for near_pairs; every row is used.
All inputs are finite; a program needn't handle non-finite values.
Results may differ from the reference program's by a relative error of at most 0.013.
Values may be sent and summed in bfloat16 or wider, within the bound.
A program may use at most 128 MiB of HBM per device.

```python
import math
import jax
import jax.numpy as jnp
import numpy as np
from jax import lax

FEATURES = 64
LEAF_SIZE = 256
SKELETON = 128
PROBES = 16
LEAF_DEV = 16
NEAR_CAP = 80
FAR_DEV = 96
SUB_LEAVES = 64
LEAVES = 8192
LEVELS = 7
N_LEAF = 128
N_SUB = 4
DEVICES = 512


def distinct_rows(key, rows, pool_size, take_count):
    row_keys = jax.random.split(key, rows)
    picked = jax.vmap(lambda row_key: jax.random.permutation(row_key, pool_size)[:take_count])(row_keys)
    return picked.astype(jnp.int32)


def pair_lists(key, count):
    span = LEAF_DEV * N_SUB - 1
    picked = distinct_rows(key, DEVICES, LEAF_DEV * span, count)
    local_leaf = picked // span
    other_leaf = picked % span
    own_index = (jnp.arange(DEVICES, dtype=jnp.int32) % N_SUB)[:, None] * LEAF_DEV + local_leaf
    partner = other_leaf + (other_leaf >= own_index).astype(jnp.int32)
    return jnp.stack([local_leaf, partner], axis=-1).astype(jnp.int32)


def draw_leaf_skel(key, part):
    return distinct_rows(jax.random.fold_in(key, 11), LEAVES, LEAF_SIZE, SKELETON)


def draw_device_skel(key, part):
    return distinct_rows(jax.random.fold_in(key, 13), DEVICES, LEAF_DEV * SKELETON, SKELETON)


def draw_subtree_skel(key, part):
    return distinct_rows(jax.random.fold_in(key, 17), N_LEAF, N_SUB * SKELETON, SKELETON)


def draw_upper_skel(key, part):
    stacked = []
    for height in range(1, LEVELS):
        node_rows = distinct_rows(jax.random.fold_in(key, 41 + height), N_LEAF >> height, 2 * SKELETON, SKELETON)
        stacked.append(jnp.repeat(node_rows, 2 ** height, axis=0))
    return jnp.stack(stacked, axis=1).astype(jnp.int32)


def draw_upper_basis(key, part):
    stacked = []
    for height in range(1, LEVELS):
        values = jax.random.normal(jax.random.fold_in(key, 71 + height), (N_LEAF >> height, SKELETON, 2 * SKELETON), jnp.float32)
        values = jnp.clip(values, -6.0, 6.0) * (1.5 * SKELETON) ** (-0.5)
        stacked.append(jnp.repeat(values, 2 ** height, axis=0))
    return jnp.stack(stacked, axis=1).astype(jnp.bfloat16)


def draw_near_pairs(key, part):
    return pair_lists(jax.random.fold_in(key, 23), NEAR_CAP)


def draw_far_pairs(key, part):
    return pair_lists(jax.random.fold_in(key, 29), FAR_DEV)


def touch_ends(result, key, low, high):
    longest = result.shape.index(max(result.shape))
    spots = []
    for shift in (0, 1):
        where = [jax.random.randint(jax.random.fold_in(key, axis), (), 0, length) for axis, length in enumerate(result.shape)]
        where[longest] = (where[longest] + shift) % result.shape[longest]
        spots.append(tuple(where))
    return result.at[spots[0]].set(low).at[spots[1]].set(high)


def level_of(key, shape, shards, low, top_value):
    loudness = 1.0
    for dim, blocks in shards:
        heights = jax.random.uniform(jax.random.fold_in(jax.random.fold_in(key, 6), dim), (blocks,), jnp.float32, low / len(shards), top_value / len(shards))
        loudness = loudness * jnp.repeat(jnp.exp(heights), shape[dim] // blocks).reshape((-1,) + (1,) * (len(shape) - 1 - dim))
    return loudness


def length_profile(number_of, total, most, lean):
    weights = [(1 << 20) // math.isqrt(rank ** lean) + 1 for rank in range(2, number_of + 1)]
    spare, given = total - most - (number_of - 1), [1] * (number_of - 1)
    while spare > 0:
        free = [i for i in range(number_of - 1) if given[i] < most]
        pool, remaining = sum([weights[i] for i in free]), spare
        for i in free:
            addition = min(most - given[i], max(1, remaining * weights[i] // pool), spare)
            given[i] = given[i] + addition
            spare = spare - addition
    return np.array([most] + given)


def uneven_parts(key, number_of, total, limit, lean):
    if number_of == 2:
        one = jax.random.randint(key, (), max(1, total - limit), min(limit, total - 1) + 1)
        return jnp.stack([one, total - one])
    tallies = jnp.asarray(length_profile(number_of, total, limit, lean), jnp.int32)
    couples = (number_of - 1) // 2
    source_of, receiver = tallies[1:1 + 2 * couples:2], tallies[2:2 + 2 * couples:2]
    room = jnp.minimum(source_of - 1, limit - receiver)
    shifted = jax.random.randint(jax.random.fold_in(key, 1), (couples,), 0, 1 << 20) % (room + 1)
    tallies = tallies.at[1:1 + 2 * couples:2].set(source_of - shifted).at[2:2 + 2 * couples:2].set(receiver + shifted)
    return tallies[jax.random.permutation(jax.random.fold_in(key, 2), number_of)]


def bell_draw(stream_key, extent, deviation, most, pieces=(), kind=jnp.bfloat16):
    values = deviation * jax.random.normal(stream_key, extent, jnp.float32)
    if pieces:
        values = values * level_of(stream_key, extent, pieces, -0.22, 0.18)
    return jnp.clip(values, -most, most).astype(kind)


def setup_inputs(seed: int = 0) -> dict:
    streams_of = jax.random.split(jax.random.key(seed), 14)
    return {
        "points": bell_draw(streams_of[0], (LEAVES, FEATURES, LEAF_SIZE), 1.0, 6.0, ((0, 512),)),
        "probe_bits": touch_ends(jax.random.randint(streams_of[1], (LEAVES, PROBES, LEAF_SIZE), 0, 2), jax.random.fold_in(streams_of[1], 1), 0, 1).astype(jnp.int32),
        "leaf_skel": draw_leaf_skel(jax.random.fold_in(streams_of[13], 71), 0),
        "leaf_basis": bell_draw(streams_of[3], (LEAVES, SKELETON, LEAF_SIZE), (SKELETON + SKELETON // 2) ** -0.5, 0.4375, ((0, 512),)),
        "device_skel": draw_device_skel(jax.random.fold_in(streams_of[13], 71), 0),
        "device_basis": bell_draw(streams_of[5], (DEVICES, SKELETON, LEAF_DEV * SKELETON), (SKELETON * (1 + LEAF_DEV // 4)) ** -0.5, 0.25, ((0, 512),)),
        "subtree_skel": draw_subtree_skel(jax.random.fold_in(streams_of[13], 71), 0),
        "subtree_basis": bell_draw(streams_of[7], (N_LEAF, SKELETON, N_SUB * SKELETON), (SKELETON * max(1, N_SUB // 2)) ** -0.5, 0.375, ((0, 128),)),
        "upper_skel": draw_upper_skel(jax.random.fold_in(streams_of[13], 71), 0),
        "upper_basis": draw_upper_basis(jax.random.fold_in(streams_of[13], 71), 0),
        "near_pairs": draw_near_pairs(jax.random.fold_in(streams_of[13], 71), 0),
        "near_count": uneven_parts(streams_of[11], DEVICES, DEVICES * NEAR_CAP * 2 // 5, NEAR_CAP, 2).astype(jnp.int32),
        "far_pairs": draw_far_pairs(jax.random.fold_in(streams_of[13], 71), 0),
    }


def kernel_tile(first_set, second_set):
    first_wide = first_set.astype(jnp.float32)
    second_wide = second_set.astype(jnp.float32)
    cross_terms = jnp.einsum('...da,...db->...ab', first_wide, second_wide)
    first_norm = jnp.sum(first_wide * first_wide, axis=-2)
    second_norm = jnp.sum(second_wide * second_wide, axis=-2)
    distance = first_norm[..., :, None] + second_norm[..., None, :] - 2.0 * cross_terms
    return jnp.exp(-distance / FEATURES).astype(jnp.bfloat16)


def joined(parts):
    shape_now = parts.shape
    moved = jnp.transpose(parts, (0, 2, 1, 3))
    return moved.reshape(shape_now[0], shape_now[2], shape_now[1] * shape_now[3])


def apply_up(weights, bases):
    return jnp.einsum('npc,nrc->npr', weights.astype(jnp.float32), bases.astype(jnp.float32)).astype(jnp.bfloat16)


def apply_down(potential, bases):
    rounded = potential.astype(jnp.bfloat16).astype(jnp.float32)
    return jnp.einsum('npr,nrc->npc', rounded, bases.astype(jnp.float32))


def select_columns(coords, skeleton):
    return jnp.take_along_axis(coords, skeleton[:, None, :].astype(jnp.int32), axis=2)


def device_terms(device_data):
    leaf_points, leaf_bits, leaf_skeleton, leaf_bases, device_skeleton, device_bases = device_data
    sign_values = (2 * leaf_bits - 1).astype(jnp.bfloat16)
    coords = select_columns(leaf_points, leaf_skeleton)
    weights = jnp.einsum('lpm,lrm->lpr', sign_values.astype(jnp.float32), leaf_bases.astype(jnp.float32)).astype(jnp.bfloat16)
    joined_weights = jnp.transpose(weights, (1, 0, 2)).reshape(PROBES, LEAF_DEV * SKELETON)
    joined_coords = jnp.transpose(coords, (1, 0, 2)).reshape(FEATURES, LEAF_DEV * SKELETON)
    node_weights = jnp.einsum('pc,rc->pr', joined_weights.astype(jnp.float32), device_bases.astype(jnp.float32)).astype(jnp.bfloat16)
    node_coords = jnp.take(joined_coords, device_skeleton.astype(jnp.int32), axis=1)
    return coords, weights, node_coords, node_weights


def subtree_terms(subtree_data):
    leaf_points, leaf_bits, leaf_bases, coords, weights, leaf_pot, near_list, counts, far_list = subtree_data
    sign_values = (2 * leaf_bits - 1).astype(jnp.bfloat16)
    signs_wide = sign_values.astype(jnp.float32)
    self_block = kernel_tile(leaf_points, leaf_points).astype(jnp.float32)
    result_sum = jnp.einsum('lpm,lmn->lpn', signs_wide, self_block)
    per_block = min(16, NEAR_CAP)
    for owner_dev in range(N_SUB):
        first_all = (owner_dev * LEAF_DEV + near_list[owner_dev, :, 0]).astype(jnp.int32)
        second_all = near_list[owner_dev, :, 1].astype(jnp.int32)
        count_now = counts[owner_dev]

        def near_step(counter, partial_value, first_all=first_all, second_all=second_all, count_now=count_now):
            slot_ids = counter * per_block + jnp.arange(per_block, dtype=jnp.int32)
            live_mask = (slot_ids < count_now).astype(jnp.float32)[:, None, None]
            slot_ids = jnp.minimum(slot_ids, NEAR_CAP - 1)
            first_leaf = first_all[slot_ids]
            second_leaf = second_all[slot_ids]
            kernel_block = kernel_tile(leaf_points[second_leaf], leaf_points[first_leaf]).astype(jnp.float32)
            to_first = jnp.einsum('fpm,fmn->fpn', signs_wide[second_leaf], kernel_block) * live_mask
            to_second = jnp.einsum('fpn,fmn->fpm', signs_wide[first_leaf], kernel_block) * live_mask
            return partial_value.at[first_leaf].add(to_first).at[second_leaf].add(to_second)

        rounds = (count_now + per_block - 1) // per_block
        result_sum = lax.fori_loop(0, rounds, near_step, result_sum)
    owner_base = jnp.arange(N_SUB, dtype=jnp.int32)[:, None] * LEAF_DEV
    far_first = (owner_base + far_list[:, :, 0]).reshape(-1).astype(jnp.int32)
    far_second = far_list[:, :, 1].reshape(-1).astype(jnp.int32)
    far_block = kernel_tile(coords[far_second], coords[far_first]).astype(jnp.float32)
    to_first_far = jnp.einsum('fpb,fba->fpa', weights[far_second].astype(jnp.float32), far_block).astype(jnp.bfloat16).astype(jnp.float32)
    to_second_far = jnp.einsum('fpa,fba->fpb', weights[far_first].astype(jnp.float32), far_block).astype(jnp.bfloat16).astype(jnp.float32)
    gathered = jnp.zeros((SUB_LEAVES, PROBES, SKELETON), jnp.float32)
    gathered = gathered.at[far_first].add(to_first_far).at[far_second].add(to_second_far)
    bases_wide = leaf_bases.astype(jnp.float32)
    result_sum = result_sum + jnp.einsum('lpr,lrm->lpm', leaf_pot.astype(jnp.bfloat16).astype(jnp.float32), bases_wide)
    result_sum = result_sum + jnp.einsum('lpr,lrm->lpm', gathered, bases_wide, precision=lax.Precision.HIGHEST)
    return result_sum


def reference(points, probe_bits, leaf_skel, leaf_basis, device_skel, device_basis, subtree_skel, subtree_basis, upper_skel, upper_basis, near_pairs, near_count, far_pairs):
    device_data = (points.reshape(DEVICES, LEAF_DEV, FEATURES, LEAF_SIZE), probe_bits.reshape(DEVICES, LEAF_DEV, PROBES, LEAF_SIZE), leaf_skel.reshape(DEVICES, LEAF_DEV, SKELETON), leaf_basis.reshape(DEVICES, LEAF_DEV, SKELETON, LEAF_SIZE), device_skel, device_basis)
    leaf_coords, leaf_weights, device_coords, device_weights = lax.map(device_terms, device_data)
    node_weights = apply_up(joined(device_weights.reshape(N_LEAF, N_SUB, PROBES, SKELETON)), subtree_basis)
    node_coords = select_columns(joined(device_coords.reshape(N_LEAF, N_SUB, FEATURES, SKELETON)), subtree_skel)
    far_terms = []
    for height in range(1, LEVELS + 1):
        left_coords, right_coords = node_coords[0::2], node_coords[1::2]
        left_weights, right_weights = node_weights[0::2], node_weights[1::2]
        kernel_block = kernel_tile(right_coords, left_coords).astype(jnp.float32)
        to_left = jnp.einsum('kpr,krl->kpl', right_weights.astype(jnp.float32), kernel_block)
        to_right = jnp.einsum('kpl,krl->kpr', left_weights.astype(jnp.float32), kernel_block)
        far_terms.append((to_left, to_right))
        if height < LEVELS:
            group_ids = jnp.arange(N_LEAF >> height, dtype=jnp.int32) * (2 ** height)
            node_weights = apply_up(jnp.concatenate([left_weights, right_weights], axis=2), upper_basis[group_ids, height - 1])
            node_coords = select_columns(jnp.concatenate([left_coords, right_coords], axis=2), upper_skel[group_ids, height - 1])
    potential = jnp.zeros((1, PROBES, SKELETON), jnp.float32)
    for height in range(LEVELS, 0, -1):
        to_left, to_right = far_terms[height - 1]
        if height < LEVELS:
            group_ids = jnp.arange(N_LEAF >> height, dtype=jnp.int32) * (2 ** height)
            spread = apply_down(potential, upper_basis[group_ids, height - 1])
            to_left = to_left + spread[:, :, :SKELETON]
            to_right = to_right + spread[:, :, SKELETON:]
        potential = jnp.stack([to_left, to_right], axis=1).reshape(-1, PROBES, SKELETON)
    sub_spread = apply_down(potential, subtree_basis)
    device_potential = jnp.transpose(sub_spread.reshape(N_LEAF, PROBES, N_SUB, SKELETON), (0, 2, 1, 3)).reshape(DEVICES, PROBES, SKELETON)
    dev_spread = apply_down(device_potential, device_basis)
    leaf_potential = jnp.transpose(dev_spread.reshape(DEVICES, PROBES, LEAF_DEV, SKELETON), (0, 2, 1, 3))
    subtree_data = (points.reshape(N_LEAF, SUB_LEAVES, FEATURES, LEAF_SIZE), probe_bits.reshape(N_LEAF, SUB_LEAVES, PROBES, LEAF_SIZE), leaf_basis.reshape(N_LEAF, SUB_LEAVES, SKELETON, LEAF_SIZE), leaf_coords.reshape(N_LEAF, SUB_LEAVES, FEATURES, SKELETON), leaf_weights.reshape(N_LEAF, SUB_LEAVES, PROBES, SKELETON), leaf_potential.reshape(N_LEAF, SUB_LEAVES, PROBES, SKELETON), near_pairs.reshape(N_LEAF, N_SUB, NEAR_CAP, 2), near_count.reshape(N_LEAF, N_SUB), far_pairs.reshape(N_LEAF, N_SUB, FAR_DEV, 2))
    results = lax.map(subtree_terms, subtree_data)
    return results.reshape(LEAVES, PROBES, LEAF_SIZE)
```

```python
import functools
import math

import jax
import jax.numpy as jnp
from jax import lax
from jax.experimental import pallas as pl
from jax.experimental.pallas import tpu as pltpu
from jax.sharding import PartitionSpec as P

F32 = jnp.float32
BF = jnp.bfloat16
I32 = jnp.int32
MESH = pl.DeviceIdType.MESH
VM = pl.BlockSpec(memory_space=pltpu.VMEM)
SM = pl.BlockSpec(memory_space=pltpu.SMEM)
NEAR_GROUP = 4
FAR_GROUP = 8
QUEUE = 256


def dot(a, b, ca=1, cb=0):
    return lax.dot_general(a, b, (((ca,), (cb,)), ((), ())), preferred_element_type=F32)


def one_hot(rows, row):
    spot = lax.broadcasted_iota(I32, (rows, row.shape[1]), 0) == row
    return jnp.where(spot, 1.0, 0.0).astype(BF)


def norm_parts(coords):
    wide = coords.astype(F32)
    norm = jnp.sum(wide * wide, axis=0, keepdims=True)
    high = norm.astype(BF).astype(F32)
    rest = norm - high
    middle = rest.astype(BF).astype(F32)
    return -high, -middle, middle - rest


def row_form(coords, parts):
    high, middle, low = parts
    at = lax.broadcasted_iota(I32, (16, coords.shape[1]), 0)
    tail = jnp.where(
        at < 3, 1.0, jnp.where(at == 3, high, jnp.where(at == 4, middle, jnp.where(at == 5, low, 0.0)))
    )
    return jnp.concatenate(
        [coords, tail.astype(BF), jnp.zeros((48, coords.shape[1]), BF)], axis=0
    )


def column_form(coords, parts):
    high, middle, low = parts
    at = lax.broadcasted_iota(I32, (16, coords.shape[1]), 0)
    tail = jnp.where(
        at == 0, high, jnp.where(at == 1, middle, jnp.where(at == 2, low, jnp.where(at < 6, 1.0, 0.0)))
    )
    return jnp.concatenate(
        [coords + coords, tail.astype(BF), jnp.zeros((48, coords.shape[1]), BF)], axis=0
    )


def tile(columns, rows, scale):
    return jnp.exp2(dot(columns, rows) * scale).astype(BF)


def upward_kernel(
    levels,
    points,
    bits,
    leaf_skel,
    leaf_basis,
    device_skel,
    device_basis,
    subtree_skel,
    subtree_basis,
    upper_skel,
    upper_basis,
    near_pairs,
    near_count,
    far_pairs,
    leaf_columns,
    leaf_rows,
    skel_columns,
    skel_rows,
    signs,
    weights,
    self_part,
    far_own,
    near_queue,
    far_queue,
    far_points,
    far_skel,
    joined,
    nodes,
    states,
    lists,
    tiles,
    near_packed,
    far_packed,
    send_sem,
    recv_sem,
    pass_sem,
    node_send,
    node_recv,
    state_send,
    state_recv,
    queue_sem,
):
    leaves, features, size = points.shape
    scale = math.log2(math.e) / features
    place = lax.axis_index("sub")
    tree = lax.axis_index("leaf")
    odd = tree & 1
    behind = (place + 3 - 2 * odd) & 3
    partners = [tree ^ (1 << t) for t in range(levels)]

    barrier = pltpu.get_barrier_semaphore()
    for k in range(1, 4):
        pl.semaphore_signal(barrier, inc=1, device_id={"sub": (place + k) & 3}, device_id_type=MESH)
    for partner in partners:
        pl.semaphore_signal(barrier, inc=1, device_id={"leaf": partner}, device_id_type=MESH)

    def make_signs(leaf, _):
        signs[leaf] = (2 * bits[leaf] - 1).astype(F32).astype(BF)
        return 0

    lax.fori_loop(0, leaves, make_signs, 0, unroll=4)
    own_list = jnp.zeros((8, 128), I32)
    lists[0] = own_list
    near_t = jnp.transpose(near_pairs[0])
    far_t = jnp.transpose(far_pairs[0])
    lists[0, 0:2, 0 : near_t.shape[1]] = near_t
    lists[0, 2:4, 0 : far_t.shape[1]] = far_t
    lists[0, 4:5, :] = jnp.full((1, 128), near_count[0], I32)

    pl.semaphore_wait(barrier, 3 + levels)

    quarter = leaves // 4

    def own_copy(k):
        if k < 4:
            part = pl.ds(k * quarter, quarter)
            pair = (points.at[part], far_points.at[0, part])
        elif k == 4:
            pair = (signs.at[pl.ds(0, leaves)], signs.at[pl.ds(leaves, leaves)])
        elif k == 5:
            pair = (leaf_skel, far_skel.at[0])
        elif k == 6:
            pair = (lists.at[0], lists.at[1])
        else:
            pair = (weights.at[pl.ds(0, leaves)], weights.at[pl.ds(leaves, leaves)])
        return pltpu.make_async_remote_copy(
            src_ref=pair[0],
            dst_ref=pair[1],
            send_sem=send_sem.at[k],
            recv_sem=recv_sem.at[k],
            device_id={"sub": behind},
            device_id_type=MESH,
        )

    def passed_copy(k):
        if k < 4:
            part = pl.ds(k * quarter, quarter)
            pair = (far_points.at[0, part], far_points.at[1, part])
        elif k == 4:
            pair = (signs.at[pl.ds(leaves, leaves)], signs.at[pl.ds(2 * leaves, leaves)])
        elif k == 5:
            pair = (far_skel.at[0], far_skel.at[1])
        else:
            pair = (weights.at[pl.ds(leaves, leaves)], weights.at[pl.ds(2 * leaves, leaves)])
        return pltpu.make_async_remote_copy(
            src_ref=pair[0],
            dst_ref=pair[1],
            send_sem=send_sem.at[8 + k],
            recv_sem=pass_sem.at[k],
            device_id={"sub": behind},
            device_id_type=MESH,
        )

    for k in (5, 6, 0, 1, 2, 3, 4):
        own_copy(k).start()

    def leaf_step(leaf, _):
        coords = points[leaf]
        parts = norm_parts(coords)
        rows = row_form(coords, parts)
        leaf_rows[leaf] = rows
        picked = dot(rows, one_hot(size, leaf_skel[pl.ds(leaf, 1), :])).astype(BF)
        skel_rows[leaf] = picked
        lane = pl.ds(pl.multiple_of(leaf * 128, 128), 128)
        joined[0:features, lane] = picked[0:features]
        weight = dot(signs[leaf], leaf_basis[leaf], 1, 1).astype(BF)
        weights[leaf] = weight
        joined[features : features + 16, lane] = weight
        return 0

    lax.fori_loop(0, leaves, leaf_step, 0, unroll=4)
    own_copy(7).start()
    nodes[place, 0:features] = dot(
        joined[0:features], one_hot(joined.shape[1], device_skel[...])
    ).astype(BF)
    nodes[place, features:] = dot(joined[features:], device_basis[0], 1, 1).astype(BF)

    def node_copy(k):
        return pltpu.make_async_remote_copy(
            src_ref=nodes.at[place],
            dst_ref=nodes.at[place],
            send_sem=node_send.at[k - 1],
            recv_sem=node_recv.at[k - 1],
            device_id={"sub": (place + k) & 3},
            device_id_type=MESH,
        )

    for k in range(1, 4):
        node_copy(k).start()

    def own_columns(leaf, _):
        coords = points[leaf]
        columns = column_form(coords, norm_parts(coords))
        leaf_columns[leaf] = jnp.transpose(columns)
        coords = skel_rows[leaf, 0:features]
        skel_columns[leaf] = jnp.transpose(column_form(coords, norm_parts(coords)))
        return 0

    def passed_columns(slot, leaf):
        columns = column_form(far_points[slot, leaf], norm_parts(far_points[slot, leaf]))
        leaf_columns[(slot + 1) * leaves + leaf] = jnp.transpose(columns)
        picked = dot(columns, one_hot(size, far_skel[slot, pl.ds(leaf, 1), :])).astype(BF)
        skel_columns[(slot + 1) * leaves + leaf] = jnp.transpose(picked)

    def columns_of(slot, first, count):
        def step(leaf, _):
            passed_columns(slot, leaf)
            return 0

        lax.fori_loop(first, first + count, step, 0, unroll=4)

    def self_blocks(first, count):
        def step(i, _):
            at = first + 4 * i
            for u in range(4):
                tiles[u] = tile(leaf_columns[at + u], leaf_rows[at + u], scale)
            for u in range(4):
                self_part[at + u] = dot(signs[at + u], tiles[u])
            return 0

        lax.fori_loop(0, count // 4, step, 0)

    def pass_on(*which):
        for k in which:
            own_copy(k).wait_recv()
            passed_copy(k).start()

    def pack_queues():
        own_copy(6).wait_recv()
        row = jnp.concatenate([lists[0], lists[1]], axis=1)
        lane = lax.broadcasted_iota(I32, (1, 256), 1)
        mine = lane < 128
        spot = lane & 127
        before = jnp.where(
            lax.broadcasted_iota(I32, (256, 256), 0) < lax.broadcasted_iota(I32, (256, 256), 1), 1.0, 0.0
        ).astype(BF)
        eight = lax.broadcasted_iota(I32, (8, 256), 0)
        for first, second, count, packed in (
            (row[0:1], row[1:2], row[4:5], near_packed),
            (row[2:3], row[3:4], far_pairs.shape[1], far_packed),
        ):
            holder = second >> 4
            slot = ((holder - place) * (1 + 2 * odd)) & 3
            wanted = jnp.where(mine, jnp.where(slot == 3, 0, 1), jnp.where(holder == place, 1, 0))
            keep = jnp.where(spot < count, wanted, 0)
            inner = jnp.where(mine, first, second & 15)
            outer = jnp.where(mine, slot * 16 + (second & 15), 16 + first) - 48
            keep_f = jnp.where(keep == 1, 1.0, 0.0)
            total = jnp.sum(keep_f, axis=1, keepdims=True)
            rank = dot(jnp.broadcast_to(keep_f, (8, 256)).astype(BF), before)[0:1]
            rank = jnp.where(keep == 1, rank, -1.0)
            chosen = jnp.where(
                lax.broadcasted_iota(I32, (QUEUE, 256), 0).astype(F32) == rank, 1.0, 0.0
            ).astype(BF)
            codes = jnp.where(eight == 0, inner, outer).astype(F32).astype(BF)
            taken = dot(codes, chosen, 1, 1)
            taken = jnp.where(eight == 0, taken, taken + 48.0)
            packed[...] = jnp.where(eight == 2, total, taken).astype(I32)
        pltpu.make_async_copy(near_packed, near_queue, queue_sem.at[0]).start()
        pltpu.make_async_copy(far_packed, far_queue, queue_sem.at[1]).start()

    def state_copy(t):
        side = (tree >> t) & 1
        return pltpu.make_async_remote_copy(
            src_ref=states.at[t, side],
            dst_ref=states.at[t, side],
            send_sem=state_send.at[t],
            recv_sem=state_recv.at[t],
            device_id={"leaf": partners[t]},
            device_id_type=MESH,
        )

    def put_state(t, state_coords, state_weights):
        side = (tree >> t) & 1
        states[t, side, 0:features] = state_coords.astype(BF)
        states[t, side, features:] = state_weights.astype(BF)
        state_copy(t).start()

    def far_term(t):
        side = (tree >> t) & 1
        mine = states[t, side, 0:features]
        other = states[t, 1 - side]
        other_coords = other[0:features]
        block = tile(
            jnp.transpose(column_form(other_coords, norm_parts(other_coords))),
            row_form(mine, norm_parts(mine)),
            scale,
        )
        far_own[t] = dot(other[features:], block)

    lax.fori_loop(0, leaves, own_columns, 0, unroll=4)
    signs[3 * leaves] = jnp.zeros_like(signs[3 * leaves])
    weights[3 * leaves] = jnp.zeros_like(weights[3 * leaves])
    leaf_columns[3 * leaves] = jnp.zeros_like(leaf_columns[3 * leaves])
    skel_columns[3 * leaves] = jnp.zeros_like(skel_columns[3 * leaves])

    for k in range(1, 4):
        node_copy(k).wait_recv()
    group = jnp.concatenate([nodes[s] for s in range(4)], axis=1)
    put_state(
        0,
        dot(group[0:features], one_hot(group.shape[1], subtree_skel[...])),
        dot(group[features:], subtree_basis[0], 1, 1),
    )

    half = leaves // 2

    def part_a():
        pass_on(5, 0, 1)
        self_blocks(0, 4)

    def part_b():
        pass_on(2, 3)
        columns_of(0, 0, half)

    def part_c():
        pack_queues()
        self_blocks(4, 4)

    def part_d():
        pass_on(4, 7)
        columns_of(0, half, half)

    def part_e():
        self_blocks(8, 8)
        passed_copy(5).wait_recv()

    def part_f():
        passed_copy(0).wait_recv()
        columns_of(1, 0, quarter)

    gaps = [part_a, part_b, part_c, part_d, part_e, part_f]
    for t in range(levels):
        if t < len(gaps):
            gaps[t]()
        state_copy(t).wait_recv()
        if t + 1 < levels:
            both = jnp.concatenate([states[t, 0], states[t, 1]], axis=1)
            put_state(
                t + 1,
                dot(both[0:features], one_hot(both.shape[1], upper_skel[0, t : t + 1, :])),
                dot(both[features:], upper_basis[0, t], 1, 1),
            )
        far_term(t)
    for gap in gaps[levels:]:
        gap()
    for k in range(1, 4):
        passed_copy(k).wait_recv()
        columns_of(1, k * quarter, quarter)
    passed_copy(4).wait_recv()
    passed_copy(7).wait_recv()

    for k in range(8):
        own_copy(k).wait_send()
        if k != 6:
            passed_copy(k).wait_send()
    for k in range(1, 4):
        node_copy(k).wait_send()
    for t in range(levels):
        state_copy(t).wait_send()
    pltpu.make_async_copy(near_packed, near_queue, queue_sem.at[0]).wait()
    pltpu.make_async_copy(far_packed, far_queue, queue_sem.at[1]).wait()


def pair_kernel(
    leaves,
    features,
    near_queue,
    far_queue,
    leaf_columns,
    leaf_rows,
    skel_columns,
    skel_rows,
    signs,
    weights,
    near_own,
    far_own,
    near_out,
    far_out,
    near_sum,
    far_sum,
    near_tiles,
    far_tiles,
):
    scale = math.log2(math.e) / features
    near_sum[...] = jnp.zeros_like(near_sum)
    far_sum[...] = jnp.zeros_like(far_sum)

    def run(queue, group, columns, rows, vectors, tiles, total, rounded):
        groups = (queue[2, 0] + 2 * group - 1) // (2 * group)

        def first_tiles():
            for u in range(group):
                tiles[0, u] = tile(columns[queue[1, u]], rows[queue[0, u]], scale)

        def half(make, to, use, source):
            found = []
            for u in range(group):
                inner = queue[0, use * group + u]
                outer = queue[1, use * group + u]
                block = tiles[source, u]
                to_inner = dot(vectors[outer], block)
                to_outer = dot(vectors[inner], block, 1, 1)
                if rounded:
                    to_inner = to_inner.astype(BF).astype(F32)
                    to_outer = to_outer.astype(BF).astype(F32)
                found.append((inner, outer, to_inner, to_outer))
                tiles[to, u] = tile(
                    columns[queue[1, make * group + u]], rows[queue[0, make * group + u]], scale
                )
            for inner, outer, to_inner, to_outer in found:
                total[inner] += to_inner
                total[outer] += to_outer

        def step(i, _):
            half(2 * i + 1, 1, 2 * i, 0)
            half(jnp.minimum(2 * i + 2, QUEUE // group - 1), 0, 2 * i + 1, 1)
            return 0

        first_tiles()
        lax.fori_loop(0, groups, step, 0)

    run(far_queue, FAR_GROUP, skel_columns, skel_rows, weights, far_tiles, far_sum, True)
    run(near_queue, NEAR_GROUP, leaf_columns, leaf_rows, signs, near_tiles, near_sum, False)
    near_own[...] = near_sum[0:leaves]
    far_own[...] = far_sum[0:leaves]
    near_out[...] = near_sum[leaves : 3 * leaves].astype(BF)
    far_out[...] = far_sum[leaves : 3 * leaves].astype(BF)


def downward_kernel(
    levels,
    near_own,
    far_leaf,
    near_out,
    far_out,
    self_part,
    far_own,
    leaf_basis,
    device_basis,
    subtree_basis,
    upper_basis,
    product,
    near_in,
    far_in,
    spread,
    send_sem,
    recv_sem,
):
    leaves = near_own.shape[0]
    place = lax.axis_index("sub")
    tree = lax.axis_index("leaf")
    odd = tree & 1
    ahead = (place + 1 + 2 * odd) & 3
    across = (place + 2) & 3
    barrier = pltpu.get_barrier_semaphore()
    for k in range(1, 4):
        pl.semaphore_signal(barrier, inc=1, device_id={"sub": (place + k) & 3}, device_id_type=MESH)
    pl.semaphore_wait(barrier, 3)

    def copy(k):
        slot, far = k // 2, k % 2
        source, target = (far_out, far_in) if far else (near_out, near_in)
        return pltpu.make_async_remote_copy(
            src_ref=source.at[pl.ds(slot * leaves, leaves)],
            dst_ref=target.at[slot],
            send_sem=send_sem.at[k],
            recv_sem=recv_sem.at[k],
            device_id={"sub": across if slot else ahead},
            device_id_type=MESH,
        )

    for k in (3, 1, 2, 0):
        copy(k).start()

    potential = far_own[levels - 1]
    for t in range(levels - 2, -1, -1):
        side = (tree >> t) & 1
        lane = pl.ds(pl.multiple_of(side * 128, 128), 128)
        potential = far_own[t] + dot(potential.astype(BF), upper_basis[0, t, :, lane])
    lane = pl.ds(pl.multiple_of(place * 128, 128), 128)
    potential = dot(potential.astype(BF), subtree_basis[0, :, lane])
    spread[...] = dot(potential.astype(BF), device_basis[0]).astype(BF)

    def tree_step(leaf, _):
        lane = pl.ds(pl.multiple_of(leaf * 128, 128), 128)
        product[leaf] = near_own[leaf] + self_part[leaf] + dot(spread[:, lane], leaf_basis[leaf])
        return 0

    lax.fori_loop(0, leaves, tree_step, 0, unroll=4)
    for k in range(4):
        copy(k).wait_recv()

    def last_step(leaf, _):
        far = far_leaf[leaf] + far_in[0, leaf].astype(F32) + far_in[1, leaf].astype(F32)
        high = far.astype(BF)
        low = (far - high.astype(F32)).astype(BF)
        both = dot(jnp.concatenate([high, low], axis=0), leaf_basis[leaf])
        near = near_in[0, leaf].astype(F32) + near_in[1, leaf].astype(F32)
        product[leaf] = product[leaf] + near + both[0:16] + both[16:32]
        return 0

    lax.fori_loop(0, leaves, last_step, 0, unroll=4)
    for k in range(4):
        copy(k).wait_send()


def on_device(
    points,
    probe_bits,
    leaf_skel,
    leaf_basis,
    device_skel,
    device_basis,
    subtree_skel,
    subtree_basis,
    upper_skel,
    upper_basis,
    near_pairs,
    near_count,
    far_pairs,
):
    leaves, features, size = points.shape
    probes = probe_bits.shape[1]
    skeleton = leaf_skel.shape[1]
    levels = upper_basis.shape[1] + 1
    known = 3 * leaves + 1
    limit = 40 << 20
    (
        leaf_columns,
        leaf_rows,
        skel_columns,
        skel_rows,
        signs,
        weights,
        self_part,
        far_own,
        near_queue,
        far_queue,
    ) = pl.pallas_call(
        functools.partial(upward_kernel, levels),
        out_shape=(
            pltpu.VMEM((known, size, 128), BF),
            pltpu.VMEM((leaves, 128, size), BF),
            pltpu.VMEM((known, skeleton, 128), BF),
            pltpu.VMEM((leaves, 128, skeleton), BF),
            pltpu.VMEM((known, probes, size), BF),
            pltpu.VMEM((known, probes, skeleton), BF),
            pltpu.VMEM((leaves, probes, size), F32),
            pltpu.VMEM((levels, probes, skeleton), F32),
            pltpu.SMEM((8, QUEUE), I32),
            pltpu.SMEM((8, QUEUE), I32),
        ),
        in_specs=[VM] * 11 + [SM, VM],
        out_specs=(VM,) * 8 + (SM, SM),
        scratch_shapes=[
            pltpu.VMEM((2, leaves, features, size), BF),
            pltpu.VMEM((2, leaves, skeleton), I32),
            pltpu.VMEM((features + probes, leaves * skeleton), BF),
            pltpu.VMEM((4, features + probes, skeleton), BF),
            pltpu.VMEM((levels, 2, features + probes, skeleton), BF),
            pltpu.VMEM((2, 8, 128), I32),
            pltpu.VMEM((4, size, size), BF),
            pltpu.VMEM((8, QUEUE), I32),
            pltpu.VMEM((8, QUEUE), I32),
            pltpu.SemaphoreType.DMA((16,)),
            pltpu.SemaphoreType.DMA((8,)),
            pltpu.SemaphoreType.DMA((8,)),
            pltpu.SemaphoreType.DMA((3,)),
            pltpu.SemaphoreType.DMA((3,)),
            pltpu.SemaphoreType.DMA((levels,)),
            pltpu.SemaphoreType.DMA((levels,)),
            pltpu.SemaphoreType.DMA((2,)),
        ],
        compiler_params=pltpu.CompilerParams(
            collective_id=1, has_side_effects=True, vmem_limit_bytes=limit
        ),
        name="upward",
    )(
        points,
        probe_bits,
        leaf_skel,
        leaf_basis,
        device_skel,
        device_basis,
        subtree_skel,
        subtree_basis,
        upper_skel,
        upper_basis,
        near_pairs,
        near_count,
        far_pairs,
    )
    near_own, far_leaf, near_out, far_out = pl.pallas_call(
        functools.partial(pair_kernel, leaves, features),
        out_shape=(
            pltpu.VMEM((leaves, probes, size), F32),
            pltpu.VMEM((leaves, probes, skeleton), F32),
            pltpu.VMEM((2 * leaves, probes, size), BF),
            pltpu.VMEM((2 * leaves, probes, skeleton), BF),
        ),
        in_specs=[SM, SM] + [VM] * 6,
        out_specs=(VM,) * 4,
        scratch_shapes=[
            pltpu.VMEM((known, probes, size), F32),
            pltpu.VMEM((known, probes, skeleton), F32),
            pltpu.VMEM((2, NEAR_GROUP, size, size), BF),
            pltpu.VMEM((2, FAR_GROUP, skeleton, skeleton), BF),
        ],
        compiler_params=pltpu.CompilerParams(vmem_limit_bytes=limit),
        name="pairs",
    )(near_queue, far_queue, leaf_columns, leaf_rows, skel_columns, skel_rows, signs, weights)
    return pl.pallas_call(
        functools.partial(downward_kernel, levels),
        out_shape=jax.ShapeDtypeStruct((leaves, probes, size), F32),
        in_specs=[VM] * 10,
        out_specs=VM,
        scratch_shapes=[
            pltpu.VMEM((2, leaves, probes, size), BF),
            pltpu.VMEM((2, leaves, probes, skeleton), BF),
            pltpu.VMEM((probes, leaves * skeleton), BF),
            pltpu.SemaphoreType.DMA((4,)),
            pltpu.SemaphoreType.DMA((4,)),
        ],
        compiler_params=pltpu.CompilerParams(
            collective_id=2, has_side_effects=True, vmem_limit_bytes=limit
        ),
        name="downward",
    )(
        near_own,
        far_leaf,
        near_out,
        far_out,
        self_part,
        far_own,
        leaf_basis,
        device_basis,
        subtree_basis,
        upper_basis,
    )


def solution(mesh):
    return jax.shard_map(
        on_device,
        mesh=mesh,
        in_specs=(
            P(("leaf", "sub"), None, None),
            P(("leaf", "sub"), None, None),
            P(("leaf", "sub"), None),
            P(("leaf", "sub"), None, None),
            P(("leaf", "sub"), None),
            P(("leaf", "sub"), None, None),
            P("leaf", None),
            P("leaf", None, None),
            P("leaf", None, None),
            P("leaf", None, None, None),
            P(("leaf", "sub"), None, None),
            P(("leaf", "sub")),
            P(("leaf", "sub"), None, None),
        ),
        out_specs=P(("leaf", "sub"), None, None),
        check_vma=False,
    )
```

```python
import functools
import math

import jax
import jax.numpy as jnp
from jax import lax
from jax.experimental import pallas as pl
from jax.experimental.pallas import tpu as pltpu
from jax.sharding import PartitionSpec as P

F32 = jnp.float32
BF = jnp.bfloat16
I32 = jnp.int32
MESH = pl.DeviceIdType.MESH
VM = pl.BlockSpec(memory_space=pltpu.VMEM)
SM = pl.BlockSpec(memory_space=pltpu.SMEM)
HB = pl.BlockSpec(memory_space=pltpu.HBM)
NEAR_GROUPS = (6, 4)
FAR_GROUPS = (12, 8)
QUEUE = 240


def dot(a, b, ca=1, cb=0):
    return lax.dot_general(a, b, (((ca,), (cb,)), ((), ())), preferred_element_type=F32)


def one_hot(rows, row):
    spot = lax.broadcasted_iota(I32, (rows, row.shape[1]), 0) == row
    return jnp.where(spot, 1.0, 0.0).astype(BF)


def norm_parts(coords):
    wide = coords.astype(F32)
    norm = jnp.sum(wide * wide, axis=0, keepdims=True)
    high = norm.astype(BF).astype(F32)
    rest = norm - high
    middle = rest.astype(BF).astype(F32)
    return -high, -middle, middle - rest


def row_form(coords, parts):
    high, middle, low = parts
    at = lax.broadcasted_iota(I32, (16, coords.shape[1]), 0)
    tail = jnp.where(
        at < 3, 1.0, jnp.where(at == 3, high, jnp.where(at == 4, middle, jnp.where(at == 5, low, 0.0)))
    )
    return jnp.concatenate(
        [coords, tail.astype(BF), jnp.zeros((48, coords.shape[1]), BF)], axis=0
    )


def column_form(coords, parts):
    high, middle, low = parts
    at = lax.broadcasted_iota(I32, (16, coords.shape[1]), 0)
    tail = jnp.where(
        at == 0, high, jnp.where(at == 1, middle, jnp.where(at == 2, low, jnp.where(at < 6, 1.0, 0.0)))
    )
    return jnp.concatenate(
        [coords + coords, tail.astype(BF), jnp.zeros((48, coords.shape[1]), BF)], axis=0
    )


def tile(columns, rows, scale):
    return jnp.exp2(dot(columns, rows) * scale).astype(BF)


def plan(levels):
    rounds, low = [], 0
    while low < levels:
        left = levels - low
        count = left if left <= 3 else 2
        rounds.append((low, count))
        low += count
    return rounds


def widths(levels):
    return [1 << (low + count - t) for low, count in plan(levels) for t in range(low, low + count)]


def upward_kernel(
    levels,
    points_in,
    bits_in,
    leaf_skel_in,
    leaf_basis_in,
    device_skel_in,
    device_basis_in,
    subtree_skel_in,
    subtree_basis_in,
    upper_skel_in,
    upper_basis_in,
    near_in,
    near_count,
    far_in,
    leaf_columns,
    leaf_rows,
    skel_columns,
    skel_rows,
    signs,
    weights,
    base,
    leaf_basis,
    queues,
    points,
    bits,
    leaf_skel,
    device_skel,
    device_basis,
    subtree_skel,
    subtree_basis,
    near_pairs,
    far_pairs,
    far_points,
    far_skel,
    joined,
    nodes,
    lists,
    tiles,
    packed,
    far_own,
    spread,
    states,
    bases,
    skels,
    hots,
    load_sem,
    send_sem,
    recv_sem,
    pass_sem,
    node_send,
    node_recv,
    state_send,
    state_recv,
    basis_send,
    basis_recv,
    queue_sem,
):
    leaves, features, size = points.shape
    scale = math.log2(math.e) / features
    place = lax.axis_index("sub")
    tree = lax.axis_index("leaf")
    odd = tree & 1
    behind = (place + 3 - 2 * odd) & 3
    rounds = plan(levels)
    wide = widths(levels)
    peers = [
        (low, m, tree ^ (m << low)) for low, count in rounds for m in range(1, 1 << count)
    ]

    barrier = pltpu.get_barrier_semaphore()
    for k in range(1, 4):
        pl.semaphore_signal(barrier, inc=1, device_id={"sub": (place + k) & 3}, device_id_type=MESH)
    for _, _, peer in peers:
        pl.semaphore_signal(barrier, inc=1, device_id={"leaf": peer}, device_id_type=MESH)

    loads = [
        (bits_in, bits),
        (near_in, near_pairs),
        (far_in, far_pairs),
        (points_in, points),
        (leaf_skel_in, leaf_skel),
        (leaf_basis_in, leaf_basis),
        (device_skel_in, device_skel),
        (device_basis_in, device_basis),
        (subtree_skel_in, subtree_skel),
        (subtree_basis_in, subtree_basis),
    ]
    for t in range(levels - 1):
        held = (tree >> (t + 1)) & (wide[t] // 2 - 1)
        loads.append((upper_basis_in.at[0, t], bases[t].at[held]))
        loads.append((upper_skel_in.at[t], skels[t].at[held]))

    def load(k):
        return pltpu.make_async_copy(loads[k][0], loads[k][1], load_sem.at[k])

    for k in range(len(loads)):
        load(k).start()

    load(0).wait()

    def make_signs(leaf, _):
        signs[leaf] = (2 * bits[leaf] - 1).astype(F32).astype(BF)
        return 0

    lax.fori_loop(0, leaves, make_signs, 0, unroll=4)
    load(1).wait()
    load(2).wait()
    lists[0] = jnp.zeros((8, 128), I32)
    lists[0, 0:2, 0 : near_pairs.shape[2]] = near_pairs[0]
    lists[0, 2:4, 0 : far_pairs.shape[2]] = far_pairs[0]
    lists[0, 4:5, :] = jnp.full((1, 128), near_count[0], I32)

    for k in range(3, len(loads)):
        load(k).wait()

    def leaf_step(leaf, _):
        coords = points[leaf]
        rows = row_form(coords, norm_parts(coords))
        leaf_rows[leaf] = rows
        picked = dot(rows, one_hot(size, leaf_skel[pl.ds(leaf, 1), :])).astype(BF)
        skel_rows[leaf] = picked
        lane = pl.ds(pl.multiple_of(leaf * 128, 128), 128)
        joined[0:features, lane] = picked[0:features]
        weight = dot(signs[leaf], leaf_basis[leaf], 1, 1).astype(BF)
        weights[leaf] = weight
        joined[features:, lane] = weight
        return 0

    lax.fori_loop(0, leaves, leaf_step, 0, unroll=4)
    pl.semaphore_wait(barrier, 3 + len(peers))

    quarter = leaves // 4

    def remote(source, target, sent, received, device):
        return pltpu.make_async_remote_copy(
            src_ref=source,
            dst_ref=target,
            send_sem=sent,
            recv_sem=received,
            device_id=device,
            device_id_type=MESH,
        )

    def own_copy(k):
        if k < 4:
            part = pl.ds(k * quarter, quarter)
            pair = (points_in.at[part], far_points.at[0, part])
        elif k == 4:
            pair = (signs.at[pl.ds(0, leaves)], signs.at[pl.ds(leaves, leaves)])
        elif k == 5:
            pair = (leaf_skel_in, far_skel.at[0])
        elif k == 6:
            pair = (lists.at[0], lists.at[1])
        else:
            pair = (weights.at[pl.ds(0, leaves)], weights.at[pl.ds(leaves, leaves)])
        return remote(*pair, send_sem.at[k], recv_sem.at[k], {"sub": behind})

    def passed_copy(k):
        if k < 4:
            part = pl.ds(k * quarter, quarter)
            pair = (far_points.at[0, part], far_points.at[1, part])
        elif k == 4:
            pair = (signs.at[pl.ds(leaves, leaves)], signs.at[pl.ds(2 * leaves, leaves)])
        elif k == 5:
            pair = (far_skel.at[0], far_skel.at[1])
        elif k == 6:
            pair = (lists.at[1], lists.at[2])
        else:
            pair = (weights.at[pl.ds(leaves, leaves)], weights.at[pl.ds(2 * leaves, leaves)])
        return remote(*pair, send_sem.at[8 + k], pass_sem.at[k], {"sub": behind})

    for k in (5, 6, 0, 1, 2, 3, 4, 7):
        own_copy(k).start()

    nodes[place, 0:features] = dot(
        joined[0:features], one_hot(joined.shape[1], device_skel[...])
    ).astype(BF)
    nodes[place, features:] = dot(joined[features:], device_basis[0], 1, 1).astype(BF)

    def node_copy(k):
        return remote(
            nodes.at[place],
            nodes.at[place],
            node_send.at[k - 1],
            node_recv.at[k - 1],
            {"sub": (place + k) & 3},
        )

    for k in range(1, 4):
        node_copy(k).start()

    basis_copies = []
    for t in range(levels - 1):
        held = (tree >> (t + 1)) & (wide[t] // 2 - 1)
        for q in range(1, wide[t] // 2):
            device = {"leaf": tree ^ (q << (t + 1))}
            for source, target in (
                (upper_basis_in.at[0, t], bases[t].at[held]),
                (upper_skel_in.at[t], skels[t].at[held]),
            ):
                n = len(basis_copies)
                basis_copies.append(
                    remote(source, target, basis_send.at[n], basis_recv.at[n], device)
                )
    for copy in basis_copies:
        copy.start()


    def own_columns(leaf, _):
        coords = points[leaf]
        leaf_columns[leaf] = jnp.transpose(column_form(coords, norm_parts(coords)))
        coords = skel_rows[leaf, 0:features]
        skel_columns[leaf] = jnp.transpose(column_form(coords, norm_parts(coords)))
        return 0

    def columns_of(slot, first, count):
        def step(leaf, _):
            coords = far_points[slot, leaf]
            columns = column_form(coords, norm_parts(coords))
            leaf_columns[(slot + 1) * leaves + leaf] = jnp.transpose(columns)
            picked = dot(columns, one_hot(size, far_skel[slot, pl.ds(leaf, 1), :])).astype(BF)
            skel_columns[(slot + 1) * leaves + leaf] = jnp.transpose(picked)
            return 0

        lax.fori_loop(first, first + count, step, 0, unroll=4)

    def self_blocks(first, count):
        def step(i, _):
            at = first + 4 * i
            for u in range(4):
                tiles[u] = tile(leaf_columns[at + u], leaf_rows[at + u], scale)
            for u in range(4):
                base[at + u] = dot(signs[at + u], tiles[u])
            return 0

        lax.fori_loop(0, count // 4, step, 0)

    def pass_on(*which):
        for k in which:
            own_copy(k).wait_recv()
            passed_copy(k).start()

    def pack_queues():
        passed_copy(6).wait_recv()
        row = jnp.concatenate([lists[0], lists[1], lists[2]], axis=1)
        lane = lax.broadcasted_iota(I32, (1, 384), 1)
        origin = lane >> 7
        spot = lane & 127
        before = jnp.where(
            lax.broadcasted_iota(I32, (384, 384), 0) < lax.broadcasted_iota(I32, (384, 384), 1), 1.0, 0.0
        ).astype(BF)
        eight = lax.broadcasted_iota(I32, (8, 384), 0)
        eight_out = lax.broadcasted_iota(I32, (8, QUEUE), 0)
        for which, first, second, count in (
            (0, row[0:1], row[1:2], row[4:5]),
            (2, row[2:3], row[3:4], far_pairs.shape[2]),
        ):
            holder = second >> 4
            slot = ((holder - place) * (1 + 2 * odd)) & 3
            inner = jnp.where(origin == 0, first, second & 15)
            outer = jnp.where(origin == 0, slot, origin) * 16
            outer = outer + jnp.where(origin == 0, second & 15, first) - 48
            here = jnp.where(slot == 0, 1, 0)
            both_sides = jnp.where(origin == 0, jnp.where(slot < 2, 1, 0), jnp.where(origin == 1, here, 0))
            one_side = jnp.where(
                origin == 0, jnp.where(slot == 2, 1, 0), jnp.where(origin == 2, here, 0)
            )
            codes = jnp.where(eight == 0, inner, outer).astype(F32).astype(BF)
            for side, wanted in enumerate((both_sides, one_side)):
                keep = jnp.where(spot < count, wanted, 0)
                keep_f = jnp.where(keep == 1, 1.0, 0.0)
                total = jnp.sum(keep_f, axis=1, keepdims=True)
                rank = dot(jnp.broadcast_to(keep_f, (8, 384)).astype(BF), before)[0:1]
                rank = jnp.where(keep == 1, rank, -1.0)
                chosen = jnp.where(
                    lax.broadcasted_iota(I32, (QUEUE, 384), 0).astype(F32) == rank, 1.0, 0.0
                ).astype(BF)
                taken = dot(codes, chosen, 1, 1)
                taken = jnp.where(eight_out == 0, taken, taken + 48.0)
                packed[which + side] = jnp.where(eight_out == 2, total, taken).astype(I32)
        pltpu.make_async_copy(packed, queues, queue_sem.at[0]).start()

    def own_state(t):
        return (tree >> t) & (wide[t] - 1)

    def state_copies(r):
        low, count = rounds[r]
        at = states[low].at[own_state(low)]
        return [
            remote(at, at, state_send.at[n], state_recv.at[n], {"leaf": peer})
            for n, (first, _, peer) in enumerate(peers)
            if first == low
        ]

    def merge(t, node, to):
        both = jnp.concatenate([states[t][2 * node], states[t][2 * node + 1]], axis=1)
        states[t + 1][to, 0:features] = dot(both[0:features], hots[t][node]).astype(BF)
        states[t + 1][to, features:] = dot(both[features:], bases[t][node], 1, 1).astype(BF)

    def far_term(t):
        mine = states[t][own_state(t), 0:features]
        other = states[t][own_state(t) ^ 1]
        other_coords = other[0:features]
        block = tile(
            jnp.transpose(column_form(other_coords, norm_parts(other_coords))),
            row_form(mine, norm_parts(mine)),
            scale,
        )
        far_own[t] = dot(other[features:], block)

    lax.fori_loop(0, leaves, own_columns, 0, unroll=4)
    signs[3 * leaves] = jnp.zeros_like(signs[3 * leaves])
    weights[3 * leaves] = jnp.zeros_like(weights[3 * leaves])
    leaf_columns[3 * leaves] = jnp.zeros_like(leaf_columns[3 * leaves])
    skel_columns[3 * leaves] = jnp.zeros_like(skel_columns[3 * leaves])
    for k in range(1, 4):
        node_copy(k).wait_recv()
    group = jnp.concatenate([nodes[s] for s in range(4)], axis=1)
    states[0][own_state(0), 0:features] = dot(
        group[0:features], one_hot(group.shape[1], subtree_skel[...])
    ).astype(BF)
    states[0][own_state(0), features:] = dot(group[features:], subtree_basis[0], 1, 1).astype(BF)

    half = leaves // 2

    def part_a():
        for copy in basis_copies:
            copy.wait_recv()
        for t in range(levels - 1):
            for node in range(wide[t] // 2):
                hots[t][node] = one_hot(2 * 128, skels[t][node])
        pass_on(5, 6, 0, 1)

    def part_b():
        for t in range(rounds[0][1]):
            far_term(t)
        self_blocks(0, half)
        pass_on(2, 3)
        columns_of(0, 0, half)
        pass_on(4, 7)

    def part_c():
        columns_of(0, half, half)
        self_blocks(half, half)
        pack_queues()
        for t in range(rounds[0][1], rounds[-1][0]):
            far_term(t)
        passed_copy(5).wait_recv()
        for k in range(4):
            passed_copy(k).wait_recv()
            columns_of(1, k * quarter, quarter)

    gaps = [part_a, part_b, part_c]
    for r, (low, count) in enumerate(rounds):
        copies = state_copies(r)
        for copy in copies:
            copy.start()
        gaps[r]()
        for copy in copies:
            copy.wait_recv()
        for t in range(low, min(low + count, levels - 1)):
            if t + 1 < low + count:
                for node in range(wide[t] // 2):
                    merge(t, node, node)
            else:
                merge(t, 0, own_state(t + 1))
    for gap in gaps[len(rounds) :]:
        gap()
    for t in range(rounds[-1][0], levels):
        far_term(t)
    potential = far_own[levels - 1]
    for t in range(levels - 2, -1, -1):
        lane = pl.ds(pl.multiple_of(((tree >> t) & 1) * 128, 128), 128)
        held = (tree >> (t + 1)) & (wide[t] // 2 - 1)
        potential = far_own[t] + dot(potential.astype(BF), bases[t][held, :, lane])
    lane = pl.ds(pl.multiple_of(place * 128, 128), 128)
    potential = dot(potential.astype(BF), subtree_basis[0, :, lane])
    spread[...] = dot(potential.astype(BF), device_basis[0]).astype(BF)

    def tree_step(leaf, _):
        lane = pl.ds(pl.multiple_of(leaf * 128, 128), 128)
        base[leaf] = base[leaf] + dot(spread[:, lane], leaf_basis[leaf])
        return 0

    lax.fori_loop(0, leaves, tree_step, 0, unroll=4)
    passed_copy(4).wait_recv()
    passed_copy(7).wait_recv()

    for k in range(8):
        own_copy(k).wait_send()
        passed_copy(k).wait_send()
    for k in range(1, 4):
        node_copy(k).wait_send()
    for copy in basis_copies:
        copy.wait_send()
    for r in range(len(rounds)):
        for copy in state_copies(r):
            copy.wait_send()
    pltpu.make_async_copy(packed, queues, queue_sem.at[0]).wait()


def pair_kernel(
    leaves,
    features,
    queues,
    leaf_columns,
    leaf_rows,
    skel_columns,
    skel_rows,
    signs,
    weights,
    near_own,
    far_own,
    near_out,
    far_out,
    near_sum,
    far_sum,
    near_tiles,
    far_tiles,
):
    scale = math.log2(math.e) / features
    for total in (near_sum, far_sum):
        total[0 : 2 * leaves] = jnp.zeros((2 * leaves,) + total.shape[1:], F32)
        total[3 * leaves] = jnp.zeros(total.shape[1:], F32)

    def run(which, group, columns, rows, vectors, tiles, total, rounded, both_sides):
        groups = (queues[which, 2, 0] + 2 * group - 1) // (2 * group)

        def make_tile(to, u, pair):
            tiles[to, u] = tile(columns[queues[which, 1, pair]], rows[queues[which, 0, pair]], scale)

        def half(make, to, use, source):
            found = []
            for u in range(group):
                inner = queues[which, 0, use * group + u]
                outer = queues[which, 1, use * group + u]
                block = tiles[source, u]
                found.append((inner, dot(vectors[outer], block)))
                if both_sides:
                    found.append((outer, dot(vectors[inner], block, 1, 1)))
                make_tile(to, u, make * group + u)
            for leaf, term in found:
                total[leaf] += term.astype(BF).astype(F32) if rounded else term

        def step(i, _):
            half(2 * i + 1, 1, 2 * i, 0)
            half(jnp.minimum(2 * i + 2, QUEUE // group - 1), 0, 2 * i + 1, 1)
            return 0

        for u in range(group):
            make_tile(0, u, u)
        lax.fori_loop(0, groups, step, 0)

    for side in range(2):
        run(
            2 + side,
            FAR_GROUPS[side],
            skel_columns,
            skel_rows,
            weights,
            far_tiles,
            far_sum,
            True,
            side == 0,
        )
        run(
            side,
            NEAR_GROUPS[side],
            leaf_columns,
            leaf_rows,
            signs,
            near_tiles,
            near_sum,
            False,
            side == 0,
        )
    near_own[...] = near_sum[0:leaves]
    far_own[...] = far_sum[0:leaves]
    near_out[...] = near_sum[leaves : 2 * leaves].astype(BF)
    far_out[...] = far_sum[leaves : 2 * leaves].astype(BF)


def return_kernel(
    near_own,
    far_leaf,
    near_out,
    far_out,
    base,
    leaf_basis,
    product,
    near_in,
    far_in,
    send_sem,
    recv_sem,
):
    leaves = near_own.shape[0]
    place = lax.axis_index("sub")
    odd = lax.axis_index("leaf") & 1
    ahead = (place + 1 + 2 * odd) & 3
    behind = (place + 3 - 2 * odd) & 3
    barrier = pltpu.get_barrier_semaphore()
    for neighbour in (ahead, behind):
        pl.semaphore_signal(barrier, inc=1, device_id={"sub": neighbour}, device_id_type=MESH)
    pl.semaphore_wait(barrier, 2)

    def copy(k):
        source, target = (near_out, near_in) if k else (far_out, far_in)
        return pltpu.make_async_remote_copy(
            src_ref=source,
            dst_ref=target,
            send_sem=send_sem.at[k],
            recv_sem=recv_sem.at[k],
            device_id={"sub": ahead},
            device_id_type=MESH,
        )

    for k in range(2):
        copy(k).start()
    for k in range(2):
        copy(k).wait_recv()

    def last_step(leaf, _):
        far = far_leaf[leaf] + far_in[leaf].astype(F32)
        high = far.astype(BF)
        low = (far - high.astype(F32)).astype(BF)
        both = dot(jnp.concatenate([high, low], axis=0), leaf_basis[leaf])
        near = near_own[leaf] + near_in[leaf].astype(F32)
        product[leaf] = base[leaf] + near + both[0:16] + both[16:32]
        return 0

    lax.fori_loop(0, leaves, last_step, 0, unroll=4)
    for k in range(2):
        copy(k).wait_send()


def on_device(
    points,
    probe_bits,
    leaf_skel,
    leaf_basis,
    device_skel,
    device_basis,
    subtree_skel,
    subtree_basis,
    upper_skel,
    upper_basis,
    near_pairs,
    near_count,
    far_pairs,
):
    leaves, features, size = points.shape
    probes = probe_bits.shape[1]
    skeleton = leaf_skel.shape[1]
    levels = upper_basis.shape[1] + 1
    known = 3 * leaves + 1
    limit = 40 << 20
    first_limit = 55 << 20
    wide = widths(levels)
    copies = 2 * sum(wide[t] // 2 - 1 for t in range(levels - 1))
    others = sum((1 << count) - 1 for _, count in plan(levels))
    node = features + probes
    (
        leaf_columns,
        leaf_rows,
        skel_columns,
        skel_rows,
        signs,
        weights,
        base,
        basis_held,
        queues,
    ) = pl.pallas_call(
        functools.partial(upward_kernel, levels),
        out_shape=(
            pltpu.VMEM((known, size, 128), BF),
            pltpu.VMEM((leaves, 128, size), BF),
            pltpu.VMEM((known, skeleton, 128), BF),
            pltpu.VMEM((leaves, 128, skeleton), BF),
            pltpu.VMEM((known, probes, size), BF),
            pltpu.VMEM((known, probes, skeleton), BF),
            pltpu.VMEM((leaves, probes, size), F32),
            pltpu.VMEM(leaf_basis.shape, BF),
            pltpu.SMEM((4, 8, QUEUE), I32),
        ),
        in_specs=[HB] * 11 + [SM, HB],
        out_specs=(VM,) * 8 + (SM,),
        scratch_shapes=[
            pltpu.VMEM(points.shape, BF),
            pltpu.VMEM(probe_bits.shape, I32),
            pltpu.VMEM(leaf_skel.shape, I32),
            pltpu.VMEM(device_skel.shape, I32),
            pltpu.VMEM(device_basis.shape, BF),
            pltpu.VMEM(subtree_skel.shape, I32),
            pltpu.VMEM(subtree_basis.shape, BF),
            pltpu.VMEM((1, 2, near_pairs.shape[1]), I32),
            pltpu.VMEM((1, 2, far_pairs.shape[1]), I32),
            pltpu.VMEM((2, leaves, features, size), BF),
            pltpu.VMEM((2, leaves, skeleton), I32),
            pltpu.VMEM((node, leaves * skeleton), BF),
            pltpu.VMEM((4, node, skeleton), BF),
            pltpu.VMEM((3, 8, 128), I32),
            pltpu.VMEM((4, size, size), BF),
            pltpu.VMEM((4, 8, QUEUE), I32),
            pltpu.VMEM((levels, probes, skeleton), F32),
            pltpu.VMEM((probes, leaves * skeleton), BF),
            [pltpu.VMEM((wide[t], node, skeleton), BF) for t in range(levels)],
            [pltpu.VMEM((wide[t] // 2, skeleton, 2 * skeleton), BF) for t in range(levels - 1)],
            [pltpu.VMEM((wide[t] // 2, 1, skeleton), I32) for t in range(levels - 1)],
            [pltpu.VMEM((wide[t] // 2, 2 * skeleton, skeleton), BF) for t in range(levels - 1)],
            pltpu.SemaphoreType.DMA((10 + 2 * (levels - 1),)),
            pltpu.SemaphoreType.DMA((16,)),
            pltpu.SemaphoreType.DMA((8,)),
            pltpu.SemaphoreType.DMA((8,)),
            pltpu.SemaphoreType.DMA((3,)),
            pltpu.SemaphoreType.DMA((3,)),
            pltpu.SemaphoreType.DMA((others,)),
            pltpu.SemaphoreType.DMA((others,)),
            pltpu.SemaphoreType.DMA((copies,)),
            pltpu.SemaphoreType.DMA((copies,)),
            pltpu.SemaphoreType.DMA((1,)),
        ],
        compiler_params=pltpu.CompilerParams(
            collective_id=1, has_side_effects=True, vmem_limit_bytes=first_limit
        ),
        name="upward",
    )(
        points,
        probe_bits,
        leaf_skel,
        leaf_basis,
        device_skel,
        device_basis,
        subtree_skel,
        subtree_basis,
        jnp.transpose(upper_skel, (1, 0, 2)),
        upper_basis,
        jnp.transpose(near_pairs, (0, 2, 1)),
        near_count,
        jnp.transpose(far_pairs, (0, 2, 1)),
    )
    near_own, far_leaf, near_out, far_out = pl.pallas_call(
        functools.partial(pair_kernel, leaves, features),
        out_shape=(
            pltpu.VMEM((leaves, probes, size), F32),
            pltpu.VMEM((leaves, probes, skeleton), F32),
            pltpu.VMEM((leaves, probes, size), BF),
            pltpu.VMEM((leaves, probes, skeleton), BF),
        ),
        in_specs=[SM] + [VM] * 6,
        out_specs=(VM,) * 4,
        scratch_shapes=[
            pltpu.VMEM((known, probes, size), F32),
            pltpu.VMEM((known, probes, skeleton), F32),
            pltpu.VMEM((2, max(NEAR_GROUPS), size, size), BF),
            pltpu.VMEM((2, max(FAR_GROUPS), skeleton, skeleton), BF),
        ],
        compiler_params=pltpu.CompilerParams(vmem_limit_bytes=limit),
        name="pairs",
    )(queues, leaf_columns, leaf_rows, skel_columns, skel_rows, signs, weights)
    return pl.pallas_call(
        return_kernel,
        out_shape=jax.ShapeDtypeStruct((leaves, probes, size), F32),
        in_specs=[VM] * 6,
        out_specs=VM,
        scratch_shapes=[
            pltpu.VMEM((leaves, probes, size), BF),
            pltpu.VMEM((leaves, probes, skeleton), BF),
            pltpu.SemaphoreType.DMA((2,)),
            pltpu.SemaphoreType.DMA((2,)),
        ],
        compiler_params=pltpu.CompilerParams(
            collective_id=2, has_side_effects=True, vmem_limit_bytes=limit
        ),
        name="returned",
    )(near_own, far_leaf, near_out, far_out, base, basis_held)


def solution(mesh):
    return jax.shard_map(
        on_device,
        mesh=mesh,
        in_specs=(
            P(("leaf", "sub"), None, None),
            P(("leaf", "sub"), None, None),
            P(("leaf", "sub"), None),
            P(("leaf", "sub"), None, None),
            P(("leaf", "sub"), None),
            P(("leaf", "sub"), None, None),
            P("leaf", None),
            P("leaf", None, None),
            P("leaf", None, None),
            P("leaf", None, None, None),
            P(("leaf", "sub"), None, None),
            P(("leaf", "sub")),
            P(("leaf", "sub"), None, None),
        ),
        out_specs=P(("leaf", "sub"), None, None),
        check_vma=False,
    )
```

```python
import functools
import math

import jax
import jax.numpy as jnp
from jax import lax
from jax.experimental import pallas as pl
from jax.experimental.pallas import tpu as pltpu
from jax.sharding import PartitionSpec as P

F32 = jnp.float32
BF = jnp.bfloat16
I32 = jnp.int32
MESH = pl.DeviceIdType.MESH
VM = pl.BlockSpec(memory_space=pltpu.VMEM)
SM = pl.BlockSpec(memory_space=pltpu.SMEM)
HB = pl.BlockSpec(memory_space=pltpu.HBM)
NEAR_GROUP, FAR_GROUP = 6, 12
NEAR_FIXED, FAR_FIXED = (48, 24), (72, 48)
QUEUE = 240


def dot(a, b, ca=1, cb=0):
    return lax.dot_general(a, b, (((ca,), (cb,)), ((), ())), preferred_element_type=F32)


def one_hot(rows, row):
    spot = lax.broadcasted_iota(I32, (rows, row.shape[1]), 0) == row
    return jnp.where(spot, 1.0, 0.0).astype(BF)


def norm_parts(coords):
    wide = coords.astype(F32)
    norm = jnp.sum(wide * wide, axis=0, keepdims=True)
    high = norm.astype(BF).astype(F32)
    rest = norm - high
    middle = rest.astype(BF).astype(F32)
    return -high, -middle, middle - rest


def row_form(coords, parts):
    high, middle, low = parts
    at = lax.broadcasted_iota(I32, (16, coords.shape[1]), 0)
    tail = jnp.where(
        at < 3, 1.0, jnp.where(at == 3, high, jnp.where(at == 4, middle, jnp.where(at == 5, low, 0.0)))
    )
    return jnp.concatenate(
        [coords, tail.astype(BF), jnp.zeros((48, coords.shape[1]), BF)], axis=0
    )


def column_form(coords, parts):
    high, middle, low = parts
    at = lax.broadcasted_iota(I32, (16, coords.shape[1]), 0)
    tail = jnp.where(
        at == 0, high, jnp.where(at == 1, middle, jnp.where(at == 2, low, jnp.where(at < 6, 1.0, 0.0)))
    )
    return jnp.concatenate(
        [coords + coords, tail.astype(BF), jnp.zeros((48, coords.shape[1]), BF)], axis=0
    )


def tile(columns, rows, scale):
    return jnp.exp2(dot(columns, rows) * scale).astype(BF)


def plan(levels):
    rounds, low = [], 0
    while low < levels:
        left = levels - low
        count = left if left <= 3 else 2
        rounds.append((low, count))
        low += count
    return rounds


def widths(levels):
    return [1 << (low + count - t) for low, count in plan(levels) for t in range(low, low + count)]


def far_between(mine, other, features):
    coords, other_coords = mine[0:features], other[0:features]
    block = tile(
        jnp.transpose(column_form(other_coords, norm_parts(other_coords))),
        row_form(coords, norm_parts(coords)),
        math.log2(math.e) / features,
    )
    return dot(other[features:], block)


def pair_groups(
    queues, which, group, first, groups, tables, tiles, scale, rounded, both_sides, emit
):
    columns, rows, inner_vectors, outer_vectors = tables

    def at(pair):
        inner = jnp.clip(queues[which, 0, pair], 0, rows.shape[0] - 1)
        outer = jnp.clip(queues[which, 1, pair], 0, columns.shape[0] - 1)
        return inner, outer

    def make_tile(to, u, pair):
        inner, outer = at(pair)
        tiles[to, u] = tile(columns[outer], rows[inner], scale)

    def half(make, to, use, source):
        found = []
        for u in range(group):
            pair = first + use * group + u
            inner, outer = at(pair)
            block = tiles[source, u]
            terms = [dot(outer_vectors[outer], block)]
            if both_sides:
                terms.append(dot(inner_vectors[inner], block, 1, 1))
            if rounded:
                terms = [term.astype(BF).astype(F32) for term in terms]
            found.append((pair, inner, outer, terms[0], terms[-1]))
            make_tile(to, u, first + make * group + u)
        for one in found:
            emit(*one)

    def step(i, _):
        half(2 * i + 1, 1, 2 * i, 0)
        half(jnp.minimum(2 * i + 2, (QUEUE - first) // group - 1), 0, 2 * i + 1, 1)
        return 0

    for u in range(group):
        make_tile(0, u, first + u)
    lax.fori_loop(0, groups, step, 0)


def upward_kernel(
    levels,
    points_in,
    bits_in,
    leaf_skel_in,
    leaf_basis_in,
    device_skel_in,
    device_basis_in,
    subtree_skel_in,
    subtree_basis_in,
    upper_skel_in,
    upper_basis_in,
    near_in,
    near_count,
    far_in,
    leaf_columns,
    far_leaf_columns,
    leaf_rows,
    skel_columns,
    far_skel_columns,
    skel_rows,
    signs,
    far_signs,
    weights,
    far_weights,
    near_terms,
    far_terms,
    base,
    leaf_basis,
    device_basis,
    subtree_basis,
    upper_basis,
    far_own,
    last_pairs,
    queues,
    points,
    bits,
    leaf_skel,
    device_skel,
    subtree_skel,
    near_pairs,
    far_pairs,
    far_points,
    far_skel,
    joined,
    nodes,
    lists,
    near_tiles,
    far_tiles,
    packed,
    states,
    bases,
    skels,
    hots,
    load_sem,
    send_sem,
    recv_sem,
    pass_sem,
    node_send,
    node_recv,
    state_send,
    state_recv,
    basis_send,
    basis_recv,
    queue_sem,
):
    leaves, features, size = points.shape
    scale = math.log2(math.e) / features
    place = lax.axis_index("sub")
    tree = lax.axis_index("leaf")
    odd = tree & 1
    behind = (place + 3 - 2 * odd) & 3
    rounds = plan(levels)
    wide = widths(levels)
    peers = [
        (low, m, tree ^ (m << low)) for low, count in rounds for m in range(1, 1 << count)
    ]

    barrier = pltpu.get_barrier_semaphore()
    for k in range(1, 4):
        pl.semaphore_signal(barrier, inc=1, device_id={"sub": (place + k) & 3}, device_id_type=MESH)
    for _, _, peer in peers:
        pl.semaphore_signal(barrier, inc=1, device_id={"leaf": peer}, device_id_type=MESH)

    loads = [
        (bits_in, bits),
        (near_in, near_pairs),
        (far_in, far_pairs),
        (points_in, points),
        (leaf_skel_in, leaf_skel),
        (leaf_basis_in, leaf_basis),
        (device_skel_in, device_skel),
        (device_basis_in, device_basis),
        (subtree_skel_in, subtree_skel),
        (subtree_basis_in, subtree_basis),
    ]
    for t in range(levels - 1):
        held = (tree >> (t + 1)) & (wide[t] // 2 - 1)
        loads.append((upper_basis_in.at[0, t], bases[t].at[held]))
        loads.append((upper_skel_in.at[t], skels[t].at[held]))
    loads.append((upper_basis_in, upper_basis))

    def load(k):
        return pltpu.make_async_copy(loads[k][0], loads[k][1], load_sem.at[k])

    for k in range(len(loads)):
        load(k).start()

    load(0).wait()

    def make_signs(leaf, _):
        signs[leaf] = (2 * bits[leaf] - 1).astype(F32).astype(BF)
        return 0

    lax.fori_loop(0, leaves, make_signs, 0, unroll=4)
    load(1).wait()
    load(2).wait()
    lists[0] = jnp.zeros((8, 128), I32)
    lists[0, 0:2, 0 : near_pairs.shape[2]] = near_pairs[0]
    lists[0, 2:4, 0 : far_pairs.shape[2]] = far_pairs[0]
    lists[0, 4:5, :] = jnp.full((1, 128), near_count[0], I32)

    for k in range(3, len(loads) - 1):
        load(k).wait()

    def leaf_step(leaf, _):
        coords = points[leaf]
        rows = row_form(coords, norm_parts(coords))
        leaf_rows[leaf] = rows
        picked = dot(rows, one_hot(size, leaf_skel[pl.ds(leaf, 1), :])).astype(BF)
        skel_rows[leaf] = picked
        lane = pl.ds(pl.multiple_of(leaf * 128, 128), 128)
        joined[0:features, lane] = picked[0:features]
        weight = dot(signs[leaf], leaf_basis[leaf], 1, 1).astype(BF)
        weights[leaf] = weight
        joined[features:, lane] = weight
        return 0

    lax.fori_loop(0, leaves, leaf_step, 0, unroll=4)
    pl.semaphore_wait(barrier, 3 + len(peers))

    quarter = leaves // 4

    def remote(source, target, sent, received, device):
        return pltpu.make_async_remote_copy(
            src_ref=source,
            dst_ref=target,
            send_sem=sent,
            recv_sem=received,
            device_id=device,
            device_id_type=MESH,
        )

    def own_copy(k):
        if k < 4:
            part = pl.ds(k * quarter, quarter)
            pair = (points_in.at[part], far_points.at[0, part])
        elif k == 4:
            pair = (signs.at[pl.ds(0, leaves)], signs.at[pl.ds(leaves, leaves)])
        elif k == 5:
            pair = (leaf_skel_in, far_skel.at[0])
        elif k == 6:
            pair = (lists.at[0], lists.at[1])
        else:
            pair = (weights.at[pl.ds(0, leaves)], weights.at[pl.ds(leaves, leaves)])
        return remote(*pair, send_sem.at[k], recv_sem.at[k], {"sub": behind})

    def passed_copy(k):
        if k < 4:
            part = pl.ds(k * quarter, quarter)
            pair = (far_points.at[0, part], far_points.at[1, part])
        elif k == 4:
            pair = (signs.at[pl.ds(leaves, leaves)], far_signs.at[pl.ds(0, leaves)])
        elif k == 5:
            pair = (far_skel.at[0], far_skel.at[1])
        elif k == 6:
            pair = (lists.at[1], lists.at[2])
        else:
            pair = (weights.at[pl.ds(leaves, leaves)], far_weights.at[pl.ds(0, leaves)])
        return remote(*pair, send_sem.at[8 + k], pass_sem.at[k], {"sub": behind})

    for k in (5, 6, 4, 7, 0, 1, 2, 3):
        own_copy(k).start()

    nodes[place, 0:features] = dot(
        joined[0:features], one_hot(joined.shape[1], device_skel[...])
    ).astype(BF)
    nodes[place, features:] = dot(joined[features:], device_basis[0], 1, 1).astype(BF)

    def node_copy(k):
        return remote(
            nodes.at[place],
            nodes.at[place],
            node_send.at[k - 1],
            node_recv.at[k - 1],
            {"sub": (place + k) & 3},
        )

    for k in range(1, 4):
        node_copy(k).start()

    basis_copies = []
    for t in range(levels - 1):
        held = (tree >> (t + 1)) & (wide[t] // 2 - 1)
        for q in range(1, wide[t] // 2):
            device = {"leaf": tree ^ (q << (t + 1))}
            for source, target in (
                (upper_basis_in.at[0, t], bases[t].at[held]),
                (upper_skel_in.at[t], skels[t].at[held]),
            ):
                n = len(basis_copies)
                basis_copies.append(
                    remote(source, target, basis_send.at[n], basis_recv.at[n], device)
                )
    for copy in basis_copies:
        copy.start()


    def own_columns(leaf, _):
        coords = points[leaf]
        leaf_columns[leaf] = jnp.transpose(column_form(coords, norm_parts(coords)))
        coords = skel_rows[leaf, 0:features]
        skel_columns[leaf] = jnp.transpose(column_form(coords, norm_parts(coords)))
        return 0

    def columns_of(slot, first, count):
        leaf_to, skel_to = (far_leaf_columns, far_skel_columns) if slot else (leaf_columns, skel_columns)
        leaf_at = 0 if slot else leaves

        def step(leaf, _):
            coords = far_points[slot, leaf]
            columns = column_form(coords, norm_parts(coords))
            leaf_to[leaf_at + leaf] = jnp.transpose(columns)
            picked = dot(columns, one_hot(size, far_skel[slot, pl.ds(leaf, 1), :])).astype(BF)
            skel_to[leaf_at + leaf] = jnp.transpose(picked)
            return 0

        lax.fori_loop(first, first + count, step, 0, unroll=4)

    def self_blocks(first, count):
        def step(i, _):
            at = first + 4 * i
            for u in range(4):
                near_tiles[0, u] = tile(leaf_columns[at + u], leaf_rows[at + u], scale)
            for u in range(4):
                base[at + u] = dot(signs[at + u], near_tiles[0, u])
            return 0

        lax.fori_loop(0, count // 4, step, 0)

    def pass_on(*which):
        for k in which:
            own_copy(k).wait_recv()
            passed_copy(k).start()

    def pack_queues():
        passed_copy(6).wait_recv()
        row = jnp.concatenate([lists[0], lists[1], lists[2]], axis=1)
        lane = lax.broadcasted_iota(I32, (1, 384), 1)
        origin = lane >> 7
        spot = lane & 127
        before = jnp.where(
            lax.broadcasted_iota(I32, (384, 384), 0) < lax.broadcasted_iota(I32, (384, 384), 1), 1.0, 0.0
        ).astype(BF)
        eight = lax.broadcasted_iota(I32, (8, 384), 0)
        eight_out = lax.broadcasted_iota(I32, (8, QUEUE), 0)
        for which, first, second, count in (
            (0, row[0:1], row[1:2], row[4:5]),
            (2, row[2:3], row[3:4], far_pairs.shape[2]),
        ):
            holder = second >> 4
            slot = ((holder - place) * (1 + 2 * odd)) & 3
            inner = jnp.where(origin == 0, first, second & 15)
            outer = jnp.where(origin == 0, second & 15, first)
            spread_out = jnp.where(origin == 0, slot, origin) * 16 + outer - 32
            here = jnp.where(slot == 0, 1, 0)
            both_sides = jnp.where(origin == 0, jnp.where(slot < 2, 1, 0), jnp.where(origin == 1, here, 0))
            one_side = jnp.where(
                origin == 0, jnp.where(slot == 2, 1, 0), jnp.where(origin == 2, here, 0)
            )
            for side, wanted in enumerate((both_sides, one_side)):
                code = outer - 16 if side else spread_out
                codes = jnp.where(eight == 0, inner, code).astype(F32).astype(BF)
                keep = jnp.where(spot < count, wanted, 0)
                keep_f = jnp.where(keep == 1, 1.0, 0.0)
                total = jnp.sum(keep_f, axis=1, keepdims=True)
                rank = dot(jnp.broadcast_to(keep_f, (8, 384)).astype(BF), before)[0:1]
                rank = jnp.where(keep == 1, rank, -1.0)
                chosen = jnp.where(
                    lax.broadcasted_iota(I32, (QUEUE, 384), 0).astype(F32) == rank, 1.0, 0.0
                ).astype(BF)
                taken = dot(codes, chosen, 1, 1)
                taken = jnp.where(eight_out == 0, taken, taken + (16.0 if side else 32.0))
                packed[which + side] = jnp.where(eight_out == 2, total, taken).astype(I32)
        pltpu.make_async_copy(packed, queues, queue_sem.at[0]).start()

    def own_state(t):
        return (tree >> t) & (wide[t] - 1)

    def state_copies(r):
        low, count = rounds[r]
        at = states[low].at[own_state(low)]
        return [
            remote(at, at, state_send.at[n], state_recv.at[n], {"leaf": peer})
            for n, (first, _, peer) in enumerate(peers)
            if first == low
        ]

    def merge(t, node, to):
        both = jnp.concatenate([states[t][2 * node], states[t][2 * node + 1]], axis=1)
        states[t + 1][to, 0:features] = dot(both[0:features], hots[t][node]).astype(BF)
        states[t + 1][to, features:] = dot(both[features:], bases[t][node], 1, 1).astype(BF)

    def far_term(t):
        far_own[t] = far_between(states[t][own_state(t)], states[t][own_state(t) ^ 1], features)

    lax.fori_loop(0, leaves, own_columns, 0, unroll=4)
    signs[2 * leaves] = jnp.zeros_like(signs[2 * leaves])
    far_signs[leaves] = jnp.zeros_like(far_signs[leaves])
    weights[2 * leaves] = jnp.zeros_like(weights[2 * leaves])
    far_weights[leaves] = jnp.zeros_like(far_weights[leaves])
    leaf_columns[2 * leaves] = jnp.zeros_like(leaf_columns[2 * leaves])
    far_leaf_columns[leaves] = jnp.zeros_like(far_leaf_columns[leaves])
    skel_columns[2 * leaves] = jnp.zeros_like(skel_columns[2 * leaves])
    far_skel_columns[leaves] = jnp.zeros_like(far_skel_columns[leaves])
    for k in range(1, 4):
        node_copy(k).wait_recv()
    group = jnp.concatenate([nodes[s] for s in range(4)], axis=1)
    states[0][own_state(0), 0:features] = dot(
        group[0:features], one_hot(group.shape[1], subtree_skel[...])
    ).astype(BF)
    states[0][own_state(0), features:] = dot(group[features:], subtree_basis[0], 1, 1).astype(BF)

    def part_a():
        for copy in basis_copies:
            copy.wait_recv()
        for t in range(levels - 1):
            for node in range(wide[t] // 2):
                hots[t][node] = one_hot(2 * 128, skels[t][node])
        self_blocks(0, quarter)
        pass_on(5, 6, 4, 7)

    def part_b():
        for t in range(rounds[0][1]):
            far_term(t)
        self_blocks(quarter, leaves - quarter)
        for k in range(2):
            pass_on(k)
            columns_of(0, k * quarter, quarter)

    def fixed_pairs(side):
        outer_signs, outer_weights = (far_signs, far_weights) if side else (signs, weights)
        outer_leaf, outer_skel = (
            (far_leaf_columns, far_skel_columns) if side else (leaf_columns, skel_columns)
        )
        for which, group, fixed, terms, rounded, tables, tiles in (
            (2, FAR_GROUP, FAR_FIXED, far_terms, True, (outer_skel, skel_rows, weights, outer_weights), far_tiles),
            (0, NEAR_GROUP, NEAR_FIXED, near_terms, False, (outer_leaf, leaf_rows, signs, outer_signs), near_tiles),
        ):

            def emit(pair, inner, outer, to_inner, to_outer):
                if side:
                    terms[2 * fixed[0] + pair] = to_inner
                else:
                    terms[2 * pair] = to_inner
                    terms[2 * pair + 1] = to_outer

            pair_groups(
                queues,
                which + side,
                group,
                0,
                fixed[side] // (2 * group),
                tables,
                tiles,
                scale,
                rounded,
                side == 0,
                emit,
            )

    def part_c():
        pack_queues()
        for k in range(2, 4):
            pass_on(k)
            columns_of(0, k * quarter, quarter)
        for t in range(rounds[0][1], rounds[-1][0]):
            far_term(t)
        pltpu.make_async_copy(packed, queues, queue_sem.at[0]).wait()
        fixed_pairs(0)
        passed_copy(5).wait_recv()
        for k in range(4):
            passed_copy(k).wait_recv()
            columns_of(1, k * quarter, quarter)
        passed_copy(4).wait_recv()
        passed_copy(7).wait_recv()
        fixed_pairs(1)

    gaps = [part_a, part_b, part_c]
    for r, (low, count) in enumerate(rounds):
        copies = state_copies(r)
        for copy in copies:
            copy.start()
        gaps[r]()
        for copy in copies:
            copy.wait_recv()
        for t in range(low, min(low + count, levels - 1)):
            if t + 1 < low + count:
                for node in range(wide[t] // 2):
                    merge(t, node, node)
            else:
                merge(t, 0, own_state(t + 1))
    for gap in gaps[len(rounds) :]:
        gap()
    for t in range(rounds[-1][0], levels):
        for other in range(2):
            last_pairs[t - rounds[-1][0], other] = states[t][own_state(t) ^ other]
    for k in range(8):
        own_copy(k).wait_send()
        passed_copy(k).wait_send()
    for k in range(1, 4):
        node_copy(k).wait_send()
    for copy in basis_copies:
        copy.wait_send()
    for r in range(len(rounds)):
        for copy in state_copies(r):
            copy.wait_send()
    load(len(loads) - 1).wait()


def pair_kernel(
    leaves,
    features,
    queues,
    leaf_columns,
    far_leaf_columns,
    leaf_rows,
    skel_columns,
    far_skel_columns,
    skel_rows,
    signs,
    far_signs,
    weights,
    far_weights,
    near_terms,
    far_terms,
    near_own,
    far_own,
    near_out,
    far_out,
    near_sum,
    far_sum,
    near_tiles,
    far_tiles,
):
    scale = math.log2(math.e) / features
    near_sum[...] = jnp.zeros_like(near_sum)
    far_sum[...] = jnp.zeros_like(far_sum)
    steps = math.gcd(*NEAR_FIXED, *FAR_FIXED)

    def add_fixed(i, _):
        for which, fixed, terms, total in (
            (0, NEAR_FIXED, near_terms, near_sum),
            (2, FAR_FIXED, far_terms, far_sum),
        ):
            share = fixed[0] // steps
            for u in range(share):
                pair = i * share + u
                total[queues[which, 0, pair]] += terms[2 * pair]
                total[queues[which, 1, pair]] += terms[2 * pair + 1]
            share = fixed[1] // steps
            for u in range(share):
                pair = i * share + u
                total[queues[which + 1, 0, pair]] += terms[2 * fixed[0] + pair]
        return 0

    lax.fori_loop(0, steps, add_fixed, 0)
    for which, group, fixed, total, rounded, tables, tiles in (
        (2, FAR_GROUP, FAR_FIXED[0], far_sum, True, (skel_columns, skel_rows, weights, weights), far_tiles),
        (3, FAR_GROUP, FAR_FIXED[1], far_sum, True, (far_skel_columns, skel_rows, weights, far_weights), far_tiles),
        (0, NEAR_GROUP, NEAR_FIXED[0], near_sum, False, (leaf_columns, leaf_rows, signs, signs), near_tiles),
        (1, NEAR_GROUP, NEAR_FIXED[1], near_sum, False, (far_leaf_columns, leaf_rows, signs, far_signs), near_tiles),
    ):
        both_sides = which % 2 == 0
        left = queues[which, 2, 0] - fixed

        @pl.when(left > 0)
        def _():
            def emit(pair, inner, outer, to_inner, to_outer):
                total[inner] += to_inner
                if both_sides:
                    total[outer] += to_outer

            pair_groups(
                queues,
                which,
                group,
                fixed,
                (left + 2 * group - 1) // (2 * group),
                tables,
                tiles,
                scale,
                rounded,
                both_sides,
                emit,
            )

    near_own[...] = near_sum[0:leaves]
    far_own[...] = far_sum[0:leaves]
    near_out[...] = near_sum[leaves : 2 * leaves].astype(BF)
    far_out[...] = far_sum[leaves : 2 * leaves].astype(BF)


def return_kernel(
    levels,
    features,
    near_own,
    far_leaf,
    near_out,
    far_out,
    base,
    leaf_basis,
    device_basis,
    subtree_basis,
    upper_basis,
    far_own,
    last_pairs,
    product,
    near_in,
    far_in,
    spread,
    send_sem,
    recv_sem,
):
    leaves = near_own.shape[0]
    place = lax.axis_index("sub")
    tree = lax.axis_index("leaf")
    odd = tree & 1
    ahead = (place + 1 + 2 * odd) & 3
    behind = (place + 3 - 2 * odd) & 3
    barrier = pltpu.get_barrier_semaphore()
    for neighbour in (ahead, behind):
        pl.semaphore_signal(barrier, inc=1, device_id={"sub": neighbour}, device_id_type=MESH)
    pl.semaphore_wait(barrier, 2)

    def copy(k):
        source, target = (near_out, near_in) if k else (far_out, far_in)
        return pltpu.make_async_remote_copy(
            src_ref=source,
            dst_ref=target,
            send_sem=send_sem.at[k],
            recv_sem=recv_sem.at[k],
            device_id={"sub": ahead},
            device_id_type=MESH,
        )

    for k in range(2):
        copy(k).start()

    first = levels - last_pairs.shape[0]
    fars = [far_own[t] for t in range(first)]
    for t in range(first, levels):
        fars.append(far_between(last_pairs[t - first, 0], last_pairs[t - first, 1], features))
    potential = fars[levels - 1]
    for t in range(levels - 2, -1, -1):
        lane = pl.ds(pl.multiple_of(((tree >> t) & 1) * 128, 128), 128)
        potential = fars[t] + dot(potential.astype(BF), upper_basis[0, t, :, lane])
    lane = pl.ds(pl.multiple_of(place * 128, 128), 128)
    potential = dot(potential.astype(BF), subtree_basis[0, :, lane])
    spread[...] = dot(potential.astype(BF), device_basis[0]).astype(BF)

    def tree_step(leaf, _):
        lane = pl.ds(pl.multiple_of(leaf * 128, 128), 128)
        near = base[leaf] + near_own[leaf]
        product[leaf] = near + dot(spread[:, lane], leaf_basis[leaf])
        return 0

    lax.fori_loop(0, leaves, tree_step, 0, unroll=4)
    for k in range(2):
        copy(k).wait_recv()

    def last_step(leaf, _):
        far = far_leaf[leaf] + far_in[leaf].astype(F32)
        high = far.astype(BF)
        low = (far - high.astype(F32)).astype(BF)
        both = dot(jnp.concatenate([high, low], axis=0), leaf_basis[leaf])
        near = product[leaf] + near_in[leaf].astype(F32)
        product[leaf] = near + both[0:16] + both[16:32]
        return 0

    lax.fori_loop(0, leaves, last_step, 0, unroll=4)
    for k in range(2):
        copy(k).wait_send()


def on_device(
    points,
    probe_bits,
    leaf_skel,
    leaf_basis,
    device_skel,
    device_basis,
    subtree_skel,
    subtree_basis,
    upper_skel,
    upper_basis,
    near_pairs,
    near_count,
    far_pairs,
):
    leaves, features, size = points.shape
    probes = probe_bits.shape[1]
    skeleton = leaf_skel.shape[1]
    levels = upper_basis.shape[1] + 1
    known = 2 * leaves + 1
    beyond = leaves + 1
    limit = 32 << 20
    first_limit = 50 << 20
    wide = widths(levels)
    copies = 2 * sum(wide[t] // 2 - 1 for t in range(levels - 1))
    others = sum((1 << count) - 1 for _, count in plan(levels))
    node = features + probes
    outs = pl.pallas_call(
        functools.partial(upward_kernel, levels),
        out_shape=(
            pltpu.VMEM((known, size, 128), BF),
            pltpu.VMEM((beyond, size, 128), BF),
            pltpu.VMEM((leaves, 128, size), BF),
            pltpu.VMEM((known, skeleton, 128), BF),
            pltpu.VMEM((beyond, skeleton, 128), BF),
            pltpu.VMEM((leaves, 128, skeleton), BF),
            pltpu.VMEM((known, probes, size), BF),
            pltpu.VMEM((beyond, probes, size), BF),
            pltpu.VMEM((known, probes, skeleton), BF),
            pltpu.VMEM((beyond, probes, skeleton), BF),
            pltpu.VMEM((2 * NEAR_FIXED[0] + NEAR_FIXED[1], probes, size), F32),
            pltpu.VMEM((2 * FAR_FIXED[0] + FAR_FIXED[1], probes, skeleton), F32),
            pltpu.VMEM((leaves, probes, size), F32),
            pltpu.VMEM(leaf_basis.shape, BF),
            pltpu.VMEM(device_basis.shape, BF),
            pltpu.VMEM(subtree_basis.shape, BF),
            pltpu.VMEM(upper_basis.shape, BF),
            pltpu.VMEM((levels, probes, skeleton), F32),
            pltpu.VMEM((plan(levels)[-1][1], 2, node, skeleton), BF),
            pltpu.SMEM((4, 8, QUEUE), I32),
        ),
        in_specs=[HB] * 11 + [SM, HB],
        out_specs=(VM,) * 19 + (SM,),
        scratch_shapes=[
            pltpu.VMEM(points.shape, BF),
            pltpu.VMEM(probe_bits.shape, I32),
            pltpu.VMEM(leaf_skel.shape, I32),
            pltpu.VMEM(device_skel.shape, I32),
            pltpu.VMEM(subtree_skel.shape, I32),
            pltpu.VMEM((1, 2, near_pairs.shape[1]), I32),
            pltpu.VMEM((1, 2, far_pairs.shape[1]), I32),
            pltpu.VMEM((2, leaves, features, size), BF),
            pltpu.VMEM((2, leaves, skeleton), I32),
            pltpu.VMEM((node, leaves * skeleton), BF),
            pltpu.VMEM((4, node, skeleton), BF),
            pltpu.VMEM((3, 8, 128), I32),
            pltpu.VMEM((2, NEAR_GROUP, size, size), BF),
            pltpu.VMEM((2, FAR_GROUP, skeleton, skeleton), BF),
            pltpu.VMEM((4, 8, QUEUE), I32),
            [pltpu.VMEM((wide[t], node, skeleton), BF) for t in range(levels)],
            [pltpu.VMEM((wide[t] // 2, skeleton, 2 * skeleton), BF) for t in range(levels - 1)],
            [pltpu.VMEM((wide[t] // 2, 1, skeleton), I32) for t in range(levels - 1)],
            [pltpu.VMEM((wide[t] // 2, 2 * skeleton, skeleton), BF) for t in range(levels - 1)],
            pltpu.SemaphoreType.DMA((11 + 2 * (levels - 1),)),
            pltpu.SemaphoreType.DMA((16,)),
            pltpu.SemaphoreType.DMA((8,)),
            pltpu.SemaphoreType.DMA((8,)),
            pltpu.SemaphoreType.DMA((3,)),
            pltpu.SemaphoreType.DMA((3,)),
            pltpu.SemaphoreType.DMA((others,)),
            pltpu.SemaphoreType.DMA((others,)),
            pltpu.SemaphoreType.DMA((copies,)),
            pltpu.SemaphoreType.DMA((copies,)),
            pltpu.SemaphoreType.DMA((1,)),
        ],
        compiler_params=pltpu.CompilerParams(
            collective_id=1, has_side_effects=True, vmem_limit_bytes=first_limit
        ),
        name="upward",
    )(
        points,
        probe_bits,
        leaf_skel,
        leaf_basis,
        device_skel,
        device_basis,
        subtree_skel,
        subtree_basis,
        jnp.transpose(upper_skel, (1, 0, 2)),
        upper_basis,
        jnp.transpose(near_pairs, (0, 2, 1)),
        near_count,
        jnp.transpose(far_pairs, (0, 2, 1)),
    )
    pair_tables, passed_on, queues = outs[:12], outs[12:19], outs[19]
    near_own, far_leaf, near_out, far_out = pl.pallas_call(
        functools.partial(pair_kernel, leaves, features),
        out_shape=(
            pltpu.VMEM((leaves, probes, size), F32),
            pltpu.VMEM((leaves, probes, skeleton), F32),
            pltpu.VMEM((leaves, probes, size), BF),
            pltpu.VMEM((leaves, probes, skeleton), BF),
        ),
        in_specs=[SM] + [VM] * 12,
        out_specs=(VM,) * 4,
        scratch_shapes=[
            pltpu.VMEM((known, probes, size), F32),
            pltpu.VMEM((known, probes, skeleton), F32),
            pltpu.VMEM((2, NEAR_GROUP, size, size), BF),
            pltpu.VMEM((2, FAR_GROUP, skeleton, skeleton), BF),
        ],
        compiler_params=pltpu.CompilerParams(vmem_limit_bytes=limit),
        name="pairs",
    )(queues, *pair_tables)
    return pl.pallas_call(
        functools.partial(return_kernel, levels, features),
        out_shape=jax.ShapeDtypeStruct((leaves, probes, size), F32),
        in_specs=[VM] * 11,
        out_specs=VM,
        scratch_shapes=[
            pltpu.VMEM((leaves, probes, size), BF),
            pltpu.VMEM((leaves, probes, skeleton), BF),
            pltpu.VMEM((probes, leaves * skeleton), BF),
            pltpu.SemaphoreType.DMA((2,)),
            pltpu.SemaphoreType.DMA((2,)),
        ],
        compiler_params=pltpu.CompilerParams(
            collective_id=2, has_side_effects=True, vmem_limit_bytes=limit
        ),
        name="returned",
    )(near_own, far_leaf, near_out, far_out, *passed_on)


def solution(mesh):
    return jax.shard_map(
        on_device,
        mesh=mesh,
        in_specs=(
            P(("leaf", "sub"), None, None),
            P(("leaf", "sub"), None, None),
            P(("leaf", "sub"), None),
            P(("leaf", "sub"), None, None),
            P(("leaf", "sub"), None),
            P(("leaf", "sub"), None, None),
            P("leaf", None),
            P("leaf", None, None),
            P("leaf", None, None),
            P("leaf", None, None, None),
            P(("leaf", "sub"), None, None),
            P(("leaf", "sub")),
            P(("leaf", "sub"), None, None),
        ),
        out_specs=P(("leaf", "sub"), None, None),
        check_vma=False,
    )
```

```python
import functools
import math

import jax
import jax.numpy as jnp
from jax import lax
from jax.experimental import pallas as pl
from jax.experimental.pallas import tpu as pltpu
from jax.sharding import PartitionSpec as P

F32 = jnp.float32
BF = jnp.bfloat16
I32 = jnp.int32
MESH = pl.DeviceIdType.MESH
VM = pl.BlockSpec(memory_space=pltpu.VMEM)
SM = pl.BlockSpec(memory_space=pltpu.SMEM)
HB = pl.BlockSpec(memory_space=pltpu.HBM)
NEAR_GROUP, FAR_GROUP = 6, 12
NEAR_FIXED, FAR_FIXED = (48, 24), (72, 48)
QUEUE = 240


def dot(a, b, ca=1, cb=0):
    return lax.dot_general(a, b, (((ca,), (cb,)), ((), ())), preferred_element_type=F32)


def one_hot(rows, row):
    spot = lax.broadcasted_iota(I32, (rows, row.shape[1]), 0) == row
    return jnp.where(spot, 1.0, 0.0).astype(BF)


def norm_parts(coords):
    wide = coords.astype(F32)
    norm = jnp.sum(wide * wide, axis=0, keepdims=True)
    high = norm.astype(BF).astype(F32)
    rest = norm - high
    middle = rest.astype(BF).astype(F32)
    return -high, -middle, middle - rest


def row_form(coords, parts):
    high, middle, low = parts
    at = lax.broadcasted_iota(I32, (16, coords.shape[1]), 0)
    tail = jnp.where(
        at < 3, 1.0, jnp.where(at == 3, high, jnp.where(at == 4, middle, jnp.where(at == 5, low, 0.0)))
    )
    return jnp.concatenate(
        [coords, tail.astype(BF), jnp.zeros((48, coords.shape[1]), BF)], axis=0
    )


def column_form(coords, parts):
    high, middle, low = parts
    at = lax.broadcasted_iota(I32, (16, coords.shape[1]), 0)
    tail = jnp.where(
        at == 0, high, jnp.where(at == 1, middle, jnp.where(at == 2, low, jnp.where(at < 6, 1.0, 0.0)))
    )
    return jnp.concatenate(
        [coords + coords, tail.astype(BF), jnp.zeros((48, coords.shape[1]), BF)], axis=0
    )


def tile(columns, rows, scale):
    return jnp.exp2(dot(columns, rows) * scale).astype(BF)


def plan(levels):
    rounds, low = [], 0
    while low < levels:
        left = levels - low
        count = left if left <= 3 else 2
        rounds.append((low, count))
        low += count
    return rounds


def widths(levels):
    return [1 << (low + count - t) for low, count in plan(levels) for t in range(low, low + count)]


def far_between(mine, other, features):
    coords, other_coords = mine[0:features], other[0:features]
    block = tile(
        jnp.transpose(column_form(other_coords, norm_parts(other_coords))),
        row_form(coords, norm_parts(coords)),
        math.log2(math.e) / features,
    )
    return dot(other[features:], block)


def pair_groups(
    queues, which, group, first, groups, tables, tiles, scale, rounded, both_sides, emit
):
    columns, rows, inner_vectors, outer_vectors = tables

    def at(pair):
        inner = jnp.clip(queues[which, 0, pair], 0, rows.shape[0] - 1)
        outer = jnp.clip(queues[which, 1, pair], 0, columns.shape[0] - 1)
        return inner, outer

    def make_tile(to, u, pair):
        inner, outer = at(pair)
        tiles[to, u] = tile(columns[outer], rows[inner], scale)

    def half(make, to, use, source):
        found = []
        for u in range(group):
            pair = first + use * group + u
            inner, outer = at(pair)
            block = tiles[source, u]
            terms = [dot(outer_vectors[outer], block)]
            if both_sides:
                terms.append(dot(inner_vectors[inner], block, 1, 1))
            if rounded:
                terms = [term.astype(BF).astype(F32) for term in terms]
            found.append((pair, inner, outer, terms[0], terms[-1]))
            if make is not None:
                make_tile(to, u, first + make * group + u)
        for one in found:
            emit(*one)

    def step(i, _):
        half(2 * i + 1, 1, 2 * i, 0)
        half(jnp.minimum(2 * i + 2, (QUEUE - first) // group - 1), 0, 2 * i + 1, 1)
        return 0

    for u in range(group):
        make_tile(0, u, first + u)
    if isinstance(groups, int):
        lax.fori_loop(0, groups - 1, step, 0)
        half(2 * groups - 1, 1, 2 * groups - 2, 0)
        half(None, 0, 2 * groups - 1, 1)
    else:
        lax.fori_loop(0, groups, step, 0)


def upward_kernel(
    levels,
    points_in,
    bits_in,
    leaf_skel_in,
    leaf_basis_in,
    device_skel_in,
    device_basis_in,
    subtree_skel_in,
    subtree_basis_in,
    upper_skel_in,
    upper_basis_in,
    near_in,
    near_count,
    far_in,
    leaf_columns,
    far_leaf_columns,
    leaf_rows,
    skel_columns,
    far_skel_columns,
    skel_rows,
    signs,
    far_signs,
    weights,
    far_weights,
    near_terms,
    far_terms,
    base,
    leaf_basis,
    device_basis,
    subtree_basis,
    upper_basis,
    far_own,
    last_pairs,
    queues,
    points,
    bits,
    leaf_skel,
    device_skel,
    subtree_skel,
    near_pairs,
    far_pairs,
    far_points,
    far_skel,
    joined,
    nodes,
    lists,
    near_tiles,
    far_tiles,
    packed,
    states,
    bases,
    skels,
    hots,
    load_sem,
    send_sem,
    recv_sem,
    pass_sem,
    node_send,
    node_recv,
    state_send,
    state_recv,
    basis_send,
    basis_recv,
    queue_sem,
):
    leaves, features, size = points.shape
    scale = math.log2(math.e) / features
    place = lax.axis_index("sub")
    tree = lax.axis_index("leaf")
    odd = tree & 1
    behind = (place + 3 - 2 * odd) & 3
    rounds = plan(levels)
    wide = widths(levels)
    peers = [
        (low, m, tree ^ (m << low)) for low, count in rounds for m in range(1, 1 << count)
    ]

    barrier = pltpu.get_barrier_semaphore()
    for k in range(1, 4):
        pl.semaphore_signal(barrier, inc=1, device_id={"sub": (place + k) & 3}, device_id_type=MESH)
    for _, _, peer in peers:
        pl.semaphore_signal(barrier, inc=1, device_id={"leaf": peer}, device_id_type=MESH)

    loads = [
        (bits_in, bits),
        (near_in, near_pairs),
        (far_in, far_pairs),
        (points_in, points),
        (leaf_skel_in, leaf_skel),
        (leaf_basis_in, leaf_basis),
        (device_skel_in, device_skel),
        (device_basis_in, device_basis),
        (subtree_skel_in, subtree_skel),
        (subtree_basis_in, subtree_basis),
    ]
    for t in range(levels - 1):
        held = (tree >> (t + 1)) & (wide[t] // 2 - 1)
        loads.append((upper_basis_in.at[0, t], bases[t].at[held]))
        loads.append((upper_skel_in.at[t], skels[t].at[held]))
    loads.append((upper_basis_in, upper_basis))

    def load(k):
        return pltpu.make_async_copy(loads[k][0], loads[k][1], load_sem.at[k])

    for k in range(len(loads)):
        load(k).start()

    load(0).wait()

    def make_signs(leaf, _):
        signs[leaf] = (2 * bits[leaf] - 1).astype(F32).astype(BF)
        return 0

    lax.fori_loop(0, leaves, make_signs, 0, unroll=4)
    load(1).wait()
    load(2).wait()
    lists[0] = jnp.zeros((8, 128), I32)
    lists[0, 0:2, 0 : near_pairs.shape[2]] = near_pairs[0]
    lists[0, 2:4, 0 : far_pairs.shape[2]] = far_pairs[0]
    lists[0, 4:5, :] = jnp.full((1, 128), near_count[0], I32)

    for k in range(3, len(loads) - 1):
        load(k).wait()

    def leaf_step(leaf, _):
        coords = points[leaf]
        rows = row_form(coords, norm_parts(coords))
        leaf_rows[leaf] = rows
        picked = dot(rows, one_hot(size, leaf_skel[pl.ds(leaf, 1), :])).astype(BF)
        skel_rows[leaf] = picked
        lane = pl.ds(pl.multiple_of(leaf * 128, 128), 128)
        joined[0:features, lane] = picked[0:features]
        weight = dot(signs[leaf], leaf_basis[leaf], 1, 1).astype(BF)
        weights[leaf] = weight
        joined[features:, lane] = weight
        return 0

    lax.fori_loop(0, leaves, leaf_step, 0, unroll=4)
    pl.semaphore_wait(barrier, 3 + len(peers))

    quarter = leaves // 4

    def remote(source, target, sent, received, device):
        return pltpu.make_async_remote_copy(
            src_ref=source,
            dst_ref=target,
            send_sem=sent,
            recv_sem=received,
            device_id=device,
            device_id_type=MESH,
        )

    def own_copy(k):
        if k < 4:
            part = pl.ds(k * quarter, quarter)
            pair = (points_in.at[part], far_points.at[0, part])
        elif k == 4:
            pair = (signs.at[pl.ds(0, leaves)], signs.at[pl.ds(leaves, leaves)])
        elif k == 5:
            pair = (leaf_skel_in, far_skel.at[0])
        elif k == 6:
            pair = (lists.at[0], lists.at[1])
        else:
            pair = (weights.at[pl.ds(0, leaves)], weights.at[pl.ds(leaves, leaves)])
        return remote(*pair, send_sem.at[k], recv_sem.at[k], {"sub": behind})

    def passed_copy(k):
        if k < 4:
            part = pl.ds(k * quarter, quarter)
            pair = (far_points.at[0, part], far_points.at[1, part])
        elif k == 4:
            pair = (signs.at[pl.ds(leaves, leaves)], far_signs.at[pl.ds(0, leaves)])
        elif k == 5:
            pair = (far_skel.at[0], far_skel.at[1])
        elif k == 6:
            pair = (lists.at[1], lists.at[2])
        else:
            pair = (weights.at[pl.ds(leaves, leaves)], far_weights.at[pl.ds(0, leaves)])
        return remote(*pair, send_sem.at[8 + k], pass_sem.at[k], {"sub": behind})

    for k in (5, 6, 4, 7, 0, 1, 2, 3):
        own_copy(k).start()

    nodes[place, 0:features] = dot(
        joined[0:features], one_hot(joined.shape[1], device_skel[...])
    ).astype(BF)
    nodes[place, features:] = dot(joined[features:], device_basis[0], 1, 1).astype(BF)

    def node_copy(k):
        return remote(
            nodes.at[place],
            nodes.at[place],
            node_send.at[k - 1],
            node_recv.at[k - 1],
            {"sub": (place + k) & 3},
        )

    for k in range(1, 4):
        node_copy(k).start()

    basis_copies = []
    for t in range(levels - 1):
        held = (tree >> (t + 1)) & (wide[t] // 2 - 1)
        for q in range(1, wide[t] // 2):
            device = {"leaf": tree ^ (q << (t + 1))}
            for source, target in (
                (upper_basis_in.at[0, t], bases[t].at[held]),
                (upper_skel_in.at[t], skels[t].at[held]),
            ):
                n = len(basis_copies)
                basis_copies.append(
                    remote(source, target, basis_send.at[n], basis_recv.at[n], device)
                )
    for copy in basis_copies:
        copy.start()


    def own_columns(leaf, _):
        coords = points[leaf]
        leaf_columns[leaf] = jnp.transpose(column_form(coords, norm_parts(coords)))
        coords = skel_rows[leaf, 0:features]
        skel_columns[leaf] = jnp.transpose(column_form(coords, norm_parts(coords)))
        return 0

    def columns_of(slot, first, count):
        leaf_to, skel_to = (far_leaf_columns, far_skel_columns) if slot else (leaf_columns, skel_columns)
        leaf_at = 0 if slot else leaves

        def step(leaf, _):
            coords = far_points[slot, leaf]
            columns = column_form(coords, norm_parts(coords))
            leaf_to[leaf_at + leaf] = jnp.transpose(columns)
            picked = dot(columns, one_hot(size, far_skel[slot, pl.ds(leaf, 1), :])).astype(BF)
            skel_to[leaf_at + leaf] = jnp.transpose(picked)
            return 0

        lax.fori_loop(first, first + count, step, 0, unroll=4)

    def self_blocks(first, count):
        def step(i, _):
            at = first + 4 * i
            for u in range(4):
                near_tiles[0, u] = tile(leaf_columns[at + u], leaf_rows[at + u], scale)
            for u in range(4):
                base[at + u] = dot(signs[at + u], near_tiles[0, u])
            return 0

        lax.fori_loop(0, count // 4, step, 0)

    def pass_on(*which):
        for k in which:
            own_copy(k).wait_recv()
            passed_copy(k).start()

    def pack_queues():
        passed_copy(6).wait_recv()
        row = jnp.concatenate([lists[0], lists[1], lists[2]], axis=1)
        lane = lax.broadcasted_iota(I32, (1, 384), 1)
        origin = lane >> 7
        spot = lane & 127
        before = jnp.where(
            lax.broadcasted_iota(I32, (384, 384), 0) < lax.broadcasted_iota(I32, (384, 384), 1), 1.0, 0.0
        ).astype(BF)
        eight = lax.broadcasted_iota(I32, (8, 384), 0)
        eight_out = lax.broadcasted_iota(I32, (8, QUEUE), 0)
        for which, first, second, count in (
            (0, row[0:1], row[1:2], row[4:5]),
            (2, row[2:3], row[3:4], far_pairs.shape[2]),
        ):
            holder = second >> 4
            slot = ((holder - place) * (1 + 2 * odd)) & 3
            inner = jnp.where(origin == 0, first, second & 15)
            outer = jnp.where(origin == 0, second & 15, first)
            spread_out = jnp.where(origin == 0, slot, origin) * 16 + outer - 32
            here = jnp.where(slot == 0, 1, 0)
            both_sides = jnp.where(origin == 0, jnp.where(slot < 2, 1, 0), jnp.where(origin == 1, here, 0))
            one_side = jnp.where(
                origin == 0, jnp.where(slot == 2, 1, 0), jnp.where(origin == 2, here, 0)
            )
            for side, wanted in enumerate((both_sides, one_side)):
                code = outer - 16 if side else spread_out
                codes = jnp.where(eight == 0, inner, code).astype(F32).astype(BF)
                keep = jnp.where(spot < count, wanted, 0)
                keep_f = jnp.where(keep == 1, 1.0, 0.0)
                total = jnp.sum(keep_f, axis=1, keepdims=True)
                rank = dot(jnp.broadcast_to(keep_f, (8, 384)).astype(BF), before)[0:1]
                rank = jnp.where(keep == 1, rank, -1.0)
                chosen = jnp.where(
                    lax.broadcasted_iota(I32, (QUEUE, 384), 0).astype(F32) == rank, 1.0, 0.0
                ).astype(BF)
                taken = dot(codes, chosen, 1, 1)
                taken = jnp.where(eight_out == 0, taken, taken + (16.0 if side else 32.0))
                packed[which + side] = jnp.where(eight_out == 2, total, taken).astype(I32)
        pltpu.make_async_copy(packed, queues, queue_sem.at[0]).start()

    def own_state(t):
        return (tree >> t) & (wide[t] - 1)

    def state_copies(r):
        low, count = rounds[r]
        at = states[low].at[own_state(low)]
        return [
            remote(at, at, state_send.at[n], state_recv.at[n], {"leaf": peer})
            for n, (first, _, peer) in enumerate(peers)
            if first == low
        ]

    def merge(t, node, to):
        both = jnp.concatenate([states[t][2 * node], states[t][2 * node + 1]], axis=1)
        states[t + 1][to, 0:features] = dot(both[0:features], hots[t][node]).astype(BF)
        states[t + 1][to, features:] = dot(both[features:], bases[t][node], 1, 1).astype(BF)

    def far_term(t):
        far_own[t] = far_between(states[t][own_state(t)], states[t][own_state(t) ^ 1], features)

    lax.fori_loop(0, leaves, own_columns, 0, unroll=4)
    signs[2 * leaves] = jnp.zeros_like(signs[2 * leaves])
    far_signs[leaves] = jnp.zeros_like(far_signs[leaves])
    weights[2 * leaves] = jnp.zeros_like(weights[2 * leaves])
    far_weights[leaves] = jnp.zeros_like(far_weights[leaves])
    leaf_columns[2 * leaves] = jnp.zeros_like(leaf_columns[2 * leaves])
    far_leaf_columns[leaves] = jnp.zeros_like(far_leaf_columns[leaves])
    skel_columns[2 * leaves] = jnp.zeros_like(skel_columns[2 * leaves])
    far_skel_columns[leaves] = jnp.zeros_like(far_skel_columns[leaves])
    for k in range(1, 4):
        node_copy(k).wait_recv()
    group = jnp.concatenate([nodes[s] for s in range(4)], axis=1)
    states[0][own_state(0), 0:features] = dot(
        group[0:features], one_hot(group.shape[1], subtree_skel[...])
    ).astype(BF)
    states[0][own_state(0), features:] = dot(group[features:], subtree_basis[0], 1, 1).astype(BF)

    def part_a():
        for copy in basis_copies:
            copy.wait_recv()
        for t in range(levels - 1):
            for node in range(wide[t] // 2):
                hots[t][node] = one_hot(2 * 128, skels[t][node])
        self_blocks(0, quarter)
        pass_on(5, 6, 4, 7)

    def part_b():
        for t in range(rounds[0][1]):
            far_term(t)
        self_blocks(quarter, leaves - quarter)
        for k in range(2):
            pass_on(k)
            columns_of(0, k * quarter, quarter)
        pack_queues()

    def fixed_pairs(side):
        outer_signs, outer_weights = (far_signs, far_weights) if side else (signs, weights)
        outer_leaf, outer_skel = (
            (far_leaf_columns, far_skel_columns) if side else (leaf_columns, skel_columns)
        )
        for which, group, fixed, terms, rounded, tables, tiles in (
            (2, FAR_GROUP, FAR_FIXED, far_terms, True, (outer_skel, skel_rows, weights, outer_weights), far_tiles),
            (0, NEAR_GROUP, NEAR_FIXED, near_terms, False, (outer_leaf, leaf_rows, signs, outer_signs), near_tiles),
        ):

            def emit(pair, inner, outer, to_inner, to_outer):
                if side:
                    terms[2 * fixed[0] + pair] = to_inner
                else:
                    terms[2 * pair] = to_inner
                    terms[2 * pair + 1] = to_outer

            pair_groups(
                queues,
                which + side,
                group,
                0,
                fixed[side] // (2 * group),
                tables,
                tiles,
                scale,
                rounded,
                side == 0,
                emit,
            )

    def part_c():
        for k in range(2, 4):
            pass_on(k)
            columns_of(0, k * quarter, quarter)
        for t in range(rounds[0][1], rounds[-1][0]):
            far_term(t)
        pltpu.make_async_copy(packed, queues, queue_sem.at[0]).wait()
        fixed_pairs(0)
        passed_copy(5).wait_recv()
        for k in range(4):
            passed_copy(k).wait_recv()
            columns_of(1, k * quarter, quarter)
        passed_copy(4).wait_recv()
        passed_copy(7).wait_recv()
        fixed_pairs(1)

    gaps = [part_a, part_b, part_c]
    for r, (low, count) in enumerate(rounds):
        copies = state_copies(r)
        for copy in copies:
            copy.start()
        gaps[r]()
        for copy in copies:
            copy.wait_recv()
        for t in range(low, min(low + count, levels - 1)):
            if t + 1 < low + count:
                for node in range(wide[t] // 2):
                    merge(t, node, node)
            else:
                merge(t, 0, own_state(t + 1))
    for gap in gaps[len(rounds) :]:
        gap()
    for t in range(rounds[-1][0], levels):
        for other in range(2):
            last_pairs[t - rounds[-1][0], other] = states[t][own_state(t) ^ other]
    for k in range(8):
        own_copy(k).wait_send()
        passed_copy(k).wait_send()
    for k in range(1, 4):
        node_copy(k).wait_send()
    for copy in basis_copies:
        copy.wait_send()
    for r in range(len(rounds)):
        for copy in state_copies(r):
            copy.wait_send()
    load(len(loads) - 1).wait()


def pair_kernel(
    leaves,
    features,
    queues,
    leaf_columns,
    far_leaf_columns,
    leaf_rows,
    skel_columns,
    far_skel_columns,
    skel_rows,
    signs,
    far_signs,
    weights,
    far_weights,
    near_terms,
    far_terms,
    near_own,
    far_own,
    near_out,
    far_out,
    near_sum,
    far_sum,
    near_tiles,
    far_tiles,
):
    scale = math.log2(math.e) / features
    near_sum[...] = jnp.zeros_like(near_sum)
    far_sum[...] = jnp.zeros_like(far_sum)
    steps = math.gcd(*NEAR_FIXED, *FAR_FIXED)

    def add_fixed(i, _):
        for which, fixed, terms, total in (
            (0, NEAR_FIXED, near_terms, near_sum),
            (2, FAR_FIXED, far_terms, far_sum),
        ):
            share = fixed[0] // steps
            for u in range(share):
                pair = i * share + u
                total[queues[which, 0, pair]] += terms[2 * pair]
                total[queues[which, 1, pair]] += terms[2 * pair + 1]
            share = fixed[1] // steps
            for u in range(share):
                pair = i * share + u
                total[queues[which + 1, 0, pair]] += terms[2 * fixed[0] + pair]
        return 0

    lax.fori_loop(0, steps, add_fixed, 0)
    for which, group, fixed, total, rounded, tables, tiles in (
        (2, FAR_GROUP, FAR_FIXED[0], far_sum, True, (skel_columns, skel_rows, weights, weights), far_tiles),
        (3, FAR_GROUP, FAR_FIXED[1], far_sum, True, (far_skel_columns, skel_rows, weights, far_weights), far_tiles),
        (0, NEAR_GROUP, NEAR_FIXED[0], near_sum, False, (leaf_columns, leaf_rows, signs, signs), near_tiles),
        (1, NEAR_GROUP, NEAR_FIXED[1], near_sum, False, (far_leaf_columns, leaf_rows, signs, far_signs), near_tiles),
    ):
        both_sides = which % 2 == 0
        left = queues[which, 2, 0] - fixed

        @pl.when(left > 0)
        def _():
            def emit(pair, inner, outer, to_inner, to_outer):
                total[inner] += to_inner
                if both_sides:
                    total[outer] += to_outer

            pair_groups(
                queues,
                which,
                group,
                fixed,
                (left + 2 * group - 1) // (2 * group),
                tables,
                tiles,
                scale,
                rounded,
                both_sides,
                emit,
            )

    near_own[...] = near_sum[0:leaves]
    far_own[...] = far_sum[0:leaves]
    near_out[...] = near_sum[leaves : 2 * leaves].astype(BF)
    far_out[...] = far_sum[leaves : 2 * leaves].astype(BF)


def return_kernel(
    levels,
    features,
    near_own,
    far_leaf,
    near_out,
    far_out,
    base,
    leaf_basis,
    device_basis,
    subtree_basis,
    upper_basis,
    far_own,
    last_pairs,
    product,
    near_in,
    far_in,
    spread,
    send_sem,
    recv_sem,
):
    leaves = near_own.shape[0]
    place = lax.axis_index("sub")
    tree = lax.axis_index("leaf")
    odd = tree & 1
    ahead = (place + 1 + 2 * odd) & 3
    behind = (place + 3 - 2 * odd) & 3
    barrier = pltpu.get_barrier_semaphore()
    for neighbour in (ahead, behind):
        pl.semaphore_signal(barrier, inc=1, device_id={"sub": neighbour}, device_id_type=MESH)
    pl.semaphore_wait(barrier, 2)

    def copy(k):
        source, target = (near_out, near_in) if k else (far_out, far_in)
        return pltpu.make_async_remote_copy(
            src_ref=source,
            dst_ref=target,
            send_sem=send_sem.at[k],
            recv_sem=recv_sem.at[k],
            device_id={"sub": ahead},
            device_id_type=MESH,
        )

    for k in range(2):
        copy(k).start()

    first = levels - last_pairs.shape[0]
    fars = [far_own[t] for t in range(first)]
    for t in range(first, levels):
        fars.append(far_between(last_pairs[t - first, 0], last_pairs[t - first, 1], features))
    potential = fars[levels - 1]
    for t in range(levels - 2, -1, -1):
        lane = pl.ds(pl.multiple_of(((tree >> t) & 1) * 128, 128), 128)
        potential = fars[t] + dot(potential.astype(BF), upper_basis[0, t, :, lane])
    lane = pl.ds(pl.multiple_of(place * 128, 128), 128)
    potential = dot(potential.astype(BF), subtree_basis[0, :, lane])
    spread[...] = dot(potential.astype(BF), device_basis[0]).astype(BF)

    def tree_step(leaf, _):
        lane = pl.ds(pl.multiple_of(leaf * 128, 128), 128)
        near = base[leaf] + near_own[leaf]
        product[leaf] = near + dot(spread[:, lane], leaf_basis[leaf])
        return 0

    lax.fori_loop(0, leaves, tree_step, 0, unroll=4)
    for k in range(2):
        copy(k).wait_recv()

    def last_step(leaf, _):
        far = far_leaf[leaf] + far_in[leaf].astype(F32)
        high = far.astype(BF)
        low = (far - high.astype(F32)).astype(BF)
        both = dot(jnp.concatenate([high, low], axis=0), leaf_basis[leaf])
        near = product[leaf] + near_in[leaf].astype(F32)
        product[leaf] = near + both[0:16] + both[16:32]
        return 0

    lax.fori_loop(0, leaves, last_step, 0, unroll=4)
    for k in range(2):
        copy(k).wait_send()


def on_device(
    points,
    probe_bits,
    leaf_skel,
    leaf_basis,
    device_skel,
    device_basis,
    subtree_skel,
    subtree_basis,
    upper_skel,
    upper_basis,
    near_pairs,
    near_count,
    far_pairs,
):
    leaves, features, size = points.shape
    probes = probe_bits.shape[1]
    skeleton = leaf_skel.shape[1]
    levels = upper_basis.shape[1] + 1
    known = 2 * leaves + 1
    beyond = leaves + 1
    limit = 32 << 20
    first_limit = 50 << 20
    wide = widths(levels)
    copies = 2 * sum(wide[t] // 2 - 1 for t in range(levels - 1))
    others = sum((1 << count) - 1 for _, count in plan(levels))
    node = features + probes
    outs = pl.pallas_call(
        functools.partial(upward_kernel, levels),
        out_shape=(
            pltpu.VMEM((known, size, 128), BF),
            pltpu.VMEM((beyond, size, 128), BF),
            pltpu.VMEM((leaves, 128, size), BF),
            pltpu.VMEM((known, skeleton, 128), BF),
            pltpu.VMEM((beyond, skeleton, 128), BF),
            pltpu.VMEM((leaves, 128, skeleton), BF),
            pltpu.VMEM((known, probes, size), BF),
            pltpu.VMEM((beyond, probes, size), BF),
            pltpu.VMEM((known, probes, skeleton), BF),
            pltpu.VMEM((beyond, probes, skeleton), BF),
            pltpu.VMEM((2 * NEAR_FIXED[0] + NEAR_FIXED[1], probes, size), F32),
            pltpu.VMEM((2 * FAR_FIXED[0] + FAR_FIXED[1], probes, skeleton), F32),
            pltpu.VMEM((leaves, probes, size), F32),
            pltpu.VMEM(leaf_basis.shape, BF),
            pltpu.VMEM(device_basis.shape, BF),
            pltpu.VMEM(subtree_basis.shape, BF),
            pltpu.VMEM(upper_basis.shape, BF),
            pltpu.VMEM((levels, probes, skeleton), F32),
            pltpu.VMEM((plan(levels)[-1][1], 2, node, skeleton), BF),
            pltpu.SMEM((4, 8, QUEUE), I32),
        ),
        in_specs=[HB] * 11 + [SM, HB],
        out_specs=(VM,) * 19 + (SM,),
        scratch_shapes=[
            pltpu.VMEM(points.shape, BF),
            pltpu.VMEM(probe_bits.shape, I32),
            pltpu.VMEM(leaf_skel.shape, I32),
            pltpu.VMEM(device_skel.shape, I32),
            pltpu.VMEM(subtree_skel.shape, I32),
            pltpu.VMEM((1, 2, near_pairs.shape[1]), I32),
            pltpu.VMEM((1, 2, far_pairs.shape[1]), I32),
            pltpu.VMEM((2, leaves, features, size), BF),
            pltpu.VMEM((2, leaves, skeleton), I32),
            pltpu.VMEM((node, leaves * skeleton), BF),
            pltpu.VMEM((4, node, skeleton), BF),
            pltpu.VMEM((3, 8, 128), I32),
            pltpu.VMEM((2, NEAR_GROUP, size, size), BF),
            pltpu.VMEM((2, FAR_GROUP, skeleton, skeleton), BF),
            pltpu.VMEM((4, 8, QUEUE), I32),
            [pltpu.VMEM((wide[t], node, skeleton), BF) for t in range(levels)],
            [pltpu.VMEM((wide[t] // 2, skeleton, 2 * skeleton), BF) for t in range(levels - 1)],
            [pltpu.VMEM((wide[t] // 2, 1, skeleton), I32) for t in range(levels - 1)],
            [pltpu.VMEM((wide[t] // 2, 2 * skeleton, skeleton), BF) for t in range(levels - 1)],
            pltpu.SemaphoreType.DMA((11 + 2 * (levels - 1),)),
            pltpu.SemaphoreType.DMA((16,)),
            pltpu.SemaphoreType.DMA((8,)),
            pltpu.SemaphoreType.DMA((8,)),
            pltpu.SemaphoreType.DMA((3,)),
            pltpu.SemaphoreType.DMA((3,)),
            pltpu.SemaphoreType.DMA((others,)),
            pltpu.SemaphoreType.DMA((others,)),
            pltpu.SemaphoreType.DMA((copies,)),
            pltpu.SemaphoreType.DMA((copies,)),
            pltpu.SemaphoreType.DMA((1,)),
        ],
        compiler_params=pltpu.CompilerParams(
            collective_id=1, has_side_effects=True, vmem_limit_bytes=first_limit
        ),
        name="upward",
    )(
        points,
        probe_bits,
        leaf_skel,
        leaf_basis,
        device_skel,
        device_basis,
        subtree_skel,
        subtree_basis,
        jnp.transpose(upper_skel, (1, 0, 2)),
        upper_basis,
        jnp.transpose(near_pairs, (0, 2, 1)),
        near_count,
        jnp.transpose(far_pairs, (0, 2, 1)),
    )
    pair_tables, passed_on, queues = outs[:12], outs[12:19], outs[19]
    near_own, far_leaf, near_out, far_out = pl.pallas_call(
        functools.partial(pair_kernel, leaves, features),
        out_shape=(
            pltpu.VMEM((leaves, probes, size), F32),
            pltpu.VMEM((leaves, probes, skeleton), F32),
            pltpu.VMEM((leaves, probes, size), BF),
            pltpu.VMEM((leaves, probes, skeleton), BF),
        ),
        in_specs=[SM] + [VM] * 12,
        out_specs=(VM,) * 4,
        scratch_shapes=[
            pltpu.VMEM((known, probes, size), F32),
            pltpu.VMEM((known, probes, skeleton), F32),
            pltpu.VMEM((2, NEAR_GROUP, size, size), BF),
            pltpu.VMEM((2, FAR_GROUP, skeleton, skeleton), BF),
        ],
        compiler_params=pltpu.CompilerParams(vmem_limit_bytes=limit),
        name="pairs",
    )(queues, *pair_tables)
    return pl.pallas_call(
        functools.partial(return_kernel, levels, features),
        out_shape=jax.ShapeDtypeStruct((leaves, probes, size), F32),
        in_specs=[VM] * 11,
        out_specs=VM,
        scratch_shapes=[
            pltpu.VMEM((leaves, probes, size), BF),
            pltpu.VMEM((leaves, probes, skeleton), BF),
            pltpu.VMEM((probes, leaves * skeleton), BF),
            pltpu.SemaphoreType.DMA((2,)),
            pltpu.SemaphoreType.DMA((2,)),
        ],
        compiler_params=pltpu.CompilerParams(
            collective_id=2, has_side_effects=True, vmem_limit_bytes=limit
        ),
        name="returned",
    )(near_own, far_leaf, near_out, far_out, *passed_on)


def solution(mesh):
    return jax.shard_map(
        on_device,
        mesh=mesh,
        in_specs=(
            P(("leaf", "sub"), None, None),
            P(("leaf", "sub"), None, None),
            P(("leaf", "sub"), None),
            P(("leaf", "sub"), None, None),
            P(("leaf", "sub"), None),
            P(("leaf", "sub"), None, None),
            P("leaf", None),
            P("leaf", None, None),
            P("leaf", None, None),
            P("leaf", None, None, None),
            P(("leaf", "sub"), None, None),
            P(("leaf", "sub")),
            P(("leaf", "sub"), None, None),
        ),
        out_specs=P(("leaf", "sub"), None, None),
        check_vma=False,
    )
```
